32 devices in a mesh: space: 16 (over z, x, core), mode: 2 (over y).
Axes of the slice: x: 2, y: 2, z: 4, core: 2. Of those that a mesh axis runs over, the one named last changes fastest.
Arguments:
- eigvecs: bfloat16 [2, 512, 12, 384], P(None, 'space'), may hold values from -0.56640625 to 0.56640625
- solutions: bfloat16 [2, 512, 12, 384], P(None, 'space', None, 'mode'), may hold values from -0.56640625 to 0.56640625
- momenta: int32 [8, 3], replicated, may hold values from -3 to 3
- gammas: int32 [4], replicated, may hold values from 0 to 15
Outputs:
- fields: float32 [12288, 2, 384], P('space', None, 'mode')
- traces: float32 [4, 4, 8, 2], replicated
The draws below stay inside these ranges and needn't reach their ends.
All inputs are finite; a program needn't handle non-finite values.
Results may differ from the reference program's by a relative error of at most 0.0029.
Values may be sent and summed in bfloat16 or wider, within the bound.
No kernel may reach another device: no remote copies, remote signals or barrier semaphores. Data moves between devices by JAX's collectives and lax.ppermute only.
A program may use at most 128 MiB of HBM per device.

```python
import math
import jax
import jax.numpy as jnp
import numpy as np
from jax import lax

NEV = 384
NMOM = 8
NG = 4
LATT = 96
SITES_DEV = 32
SITES = 512


def with_ends(drawn, rng, smallest, high):
    spot = [jax.random.randint(jax.random.fold_in(rng, axis), (), 0, length) for axis, length in enumerate(drawn.shape)]
    main_axis = drawn.shape.index(max(drawn.shape))
    next_to = spot[:main_axis] + [(spot[main_axis] + 1) % drawn.shape[main_axis]] + spot[main_axis + 1:]
    return drawn.at[tuple(spot)].set(smallest).at[tuple(next_to)].set(high)


def steps_of(own_key, shape, split, least, top_value):
    def one(dim, parts):
        steps = jax.random.uniform(jax.random.fold_in(jax.random.fold_in(own_key, 6), dim), (parts,), jnp.float32, least / len(split), top_value / len(split))
        return jnp.repeat(jnp.exp(steps), shape[dim] // parts).reshape((-1,) + (1,) * (len(shape) - dim - 1))

    gain = one(*split[0])
    for cut in split[1:]:
        gain = gain * one(*cut)
    return gain


def bell_draw(rng, dims, scale, reach, cuts=(), held_as=jnp.bfloat16):
    values = jax.random.normal(rng, dims, jnp.float32) * scale
    if len(cuts) > 0:
        values = steps_of(rng, dims, cuts, -0.22, 0.18) * values
    return jnp.clip(values, min=-reach, max=reach).astype(held_as)


def setup_inputs(seed: int = 0) -> dict:
    splits = jax.random.split(jax.random.key(seed), 5)
    return {
        "eigvecs": bell_draw(splits[0], (2, SITES, 12, NEV), ((24 * SITES) ** -0.25), 0.56640625, ((1, 16),)),
        "solutions": bell_draw(splits[1], (2, SITES, 12, NEV), ((24 * SITES) ** -0.25), 0.56640625, ((1, 16), (3, 2))),
        "momenta": with_ends(jax.random.randint(splits[2], (NMOM, 3), -3, 4), jax.random.fold_in(splits[2], 1), -3, 3).astype(jnp.int32),
        "gammas": with_ends(jax.random.randint(splits[3], (NG,), 0, 16), jax.random.fold_in(splits[3], 1), 0, 15).astype(jnp.int32),
    }


def gamma_table():
    unit = 1j
    first = np.array([[0, 0, 0, unit], [0, 0, unit, 0], [0, -unit, 0, 0], [-unit, 0, 0, 0]])
    second = np.array([[0, 0, 0, -1], [0, 0, 1, 0], [0, 1, 0, 0], [-1, 0, 0, 0]], dtype=complex)
    third = np.array([[0, 0, unit, 0], [0, 0, 0, -unit], [-unit, 0, 0, 0], [0, unit, 0, 0]])
    fourth = np.array([[0, 0, 1, 0], [0, 0, 0, 1], [1, 0, 0, 0], [0, 1, 0, 0]], dtype=complex)
    basis = [first, second, third, fourth]
    table = []
    for number in range(16):
        matrix = np.eye(4, dtype=complex)
        for bit_pos in range(4):
            if (number >> bit_pos) & 1:
                matrix = matrix @ basis[bit_pos]
        table.append(matrix)
    table = np.stack(table)
    return table.real.astype(np.float32), table.imag.astype(np.float32)


def select_gammas(gammas):
    table_re, table_im = gamma_table()
    select = (gammas[:, None] == jnp.arange(16, dtype=jnp.int32)[None, :]).astype(jnp.float32)
    count = gammas.shape[0]
    real_part = jnp.dot(select, jnp.asarray(table_re).reshape(16, 16), precision=lax.Precision.HIGHEST).reshape(count, 4, 4)
    imag_part = jnp.dot(select, jnp.asarray(table_im).reshape(16, 16), precision=lax.Precision.HIGHEST).reshape(count, 4, 4)
    return real_part, imag_part


def phases(momenta, first_site, count):
    index = first_site + jnp.arange(count, dtype=jnp.int32)
    coord_x = index // (LATT * LATT)
    coord_y = (index // LATT) % LATT
    coord_z = index % LATT
    phase_int = (momenta[:, 0:1] * coord_x[None, :] + momenta[:, 1:2] * coord_y[None, :] + momenta[:, 2:3] * coord_z[None, :]) % LATT
    theta = (2.0 * math.pi / LATT) * phase_int.astype(jnp.float32)
    return jnp.cos(theta), jnp.sin(theta)


def left_side(vectors, cosine, sine_part):
    vec_re = vectors[0].astype(jnp.float32)[None]
    vec_im = vectors[1].astype(jnp.float32)[None]
    cosine = cosine[:, :, None, None]
    sine_part = sine_part[:, :, None, None]
    left_re = cosine * vec_re - sine_part * vec_im
    left_im = -(sine_part * vec_re + cosine * vec_im)
    return jnp.stack([left_re, left_im], 1).astype(jnp.bfloat16)


def right_side(vectors, gamma_re, gamma_im):
    count = vectors.shape[1]
    width = vectors.shape[3]
    sol_re = vectors[0].astype(jnp.float32).reshape(count, 4, 3, width)
    sol_im = vectors[1].astype(jnp.float32).reshape(count, 4, 3, width)
    high = lax.Precision.HIGHEST
    rot_re = jnp.einsum('gst,xtcj->gxscj', gamma_re, sol_re, precision=high) - jnp.einsum('gst,xtcj->gxscj', gamma_im, sol_im, precision=high)
    rot_im = jnp.einsum('gst,xtcj->gxscj', gamma_re, sol_im, precision=high) + jnp.einsum('gst,xtcj->gxscj', gamma_im, sol_re, precision=high)
    groups = gamma_re.shape[0]
    rot_re = rot_re.reshape(groups, count, 12, width)
    rot_im = rot_im.reshape(groups, count, 12, width)
    upper = jnp.stack([rot_re, rot_im], 3)
    lower = jnp.stack([-rot_im, rot_re], 3)
    return jnp.stack([upper, lower], 1).astype(jnp.bfloat16)


def block_term(eig_block, sol_block, momenta, gamma_re, gamma_im, first_site):
    cosine, sine_part = phases(momenta, first_site, eig_block.shape[1])
    left = left_side(eig_block, cosine, sine_part)
    right = right_side(sol_block, gamma_re, gamma_im)
    return jnp.einsum('paxci,gaxcrj->gpirj', left, right, preferred_element_type=jnp.float32)


def reference(eigvecs, solutions, momenta, gammas):
    gamma_re, gamma_im = select_gammas(gammas)
    block = SITES_DEV * 8
    blocks = SITES // block

    def add_block(number, total):
        first_site = (number * block).astype(jnp.int32)
        eig_block = lax.dynamic_slice_in_dim(eigvecs, first_site, block, 1)
        sol_block = lax.dynamic_slice_in_dim(solutions, first_site, block, 1)
        return total + block_term(eig_block, sol_block, momenta, gamma_re, gamma_im, first_site)

    start = jnp.zeros((NG, NMOM, NEV, 2, NEV), jnp.float32)
    total = lax.fori_loop(0, blocks, add_block, start)
    high = lax.Precision.HIGHEST
    mat_re = total[:, :, :, 0, :]
    mat_im = total[:, :, :, 1, :]
    trace_re = jnp.einsum('gpij,hpij->ghp', mat_re, mat_re, precision=high) + jnp.einsum('gpij,hpij->ghp', mat_im, mat_im, precision=high)
    trace_im = jnp.einsum('gpij,hpij->ghp', mat_im, mat_re, precision=high) - jnp.einsum('gpij,hpij->ghp', mat_re, mat_im, precision=high)
    traces = jnp.stack([trace_re, trace_im], -1) / float(NEV * NEV)
    fields = total.reshape(NG * NMOM * NEV, 2, NEV)
    return fields, traces
```

```python
import functools
import math

import jax
import jax.numpy as jnp
import numpy as np
from jax import lax
from jax.experimental import pallas as pl
from jax.experimental.pallas import tpu as pltpu
from jax.sharding import Mesh
from jax.sharding import PartitionSpec as P

LATT = 96
VMEM = pl.BlockSpec(memory_space=pltpu.VMEM)
SMEM = pl.BlockSpec(memory_space=pltpu.SMEM)
BF16 = jnp.bfloat16
F32 = jnp.float32


def gamma_table():
    unit = 1j
    first = np.array([[0, 0, 0, unit], [0, 0, unit, 0], [0, -unit, 0, 0], [-unit, 0, 0, 0]])
    second = np.array([[0, 0, 0, -1], [0, 0, 1, 0], [0, 1, 0, 0], [-1, 0, 0, 0]], dtype=complex)
    third = np.array([[0, 0, unit, 0], [0, 0, 0, -unit], [-unit, 0, 0, 0], [0, unit, 0, 0]])
    fourth = np.array([[0, 0, 1, 0], [0, 0, 0, 1], [1, 0, 0, 0], [0, 1, 0, 0]], dtype=complex)
    basis = [first, second, third, fourth]
    table = []
    for number in range(16):
        matrix = np.eye(4, dtype=complex)
        for bit_pos in range(4):
            if number >> bit_pos & 1:
                matrix = matrix @ basis[bit_pos]
        table.append(matrix)
    return np.stack(table)


def shift_lanes(x, by):
    by = by % x.shape[-1]
    return x if by == 0 else pltpu.roll(x, by, x.ndim - 1)


def prepare_kernel(place, eig, sol, *rest):
    eig_out, sol_out = rest[:4], rest[4:8]
    packs, turned = rest[8:]
    z, spot, half = place[0], place[1], place[2]
    start = pl.multiple_of(half * 192, 192)
    parts = [
        eig[0, pl.ds(start, 96), :].astype(F32),
        eig[1, pl.ds(start, 96), :].astype(F32),
        eig[0, pl.ds(start + 96, 96), :].astype(F32),
        eig[1, pl.ds(start + 96, 96), :].astype(F32),
    ]
    lane = lax.broadcasted_iota(jnp.int32, (96, 384), 1)
    for quarter in range(4):
        moved = [shift_lanes(part, 96 * (k - quarter)) for k, part in enumerate(parts)]
        packs[quarter] = jnp.where(
            lane < 192,
            jnp.where(lane < 96, moved[0], moved[1]),
            jnp.where(lane < 288, moved[2], moved[3]),
        ).astype(BF16)
    for k in range(4):
        eig_out[k][...] = packs[z ^ k]
    for r in range(2):
        flipped = sol[r].astype(F32).T.astype(BF16)
        for k in range(4):
            turned[k, :, r * 384 : (r + 1) * 384] = flipped[k * 48 : (k + 1) * 48]
    for k in range(4):
        sol_out[k][...] = turned[spot ^ k]


def prepare(place, eig, sol):
    return pl.pallas_call(
        prepare_kernel,
        out_shape=[jax.ShapeDtypeStruct((96, 384), BF16)] * 4
        + [jax.ShapeDtypeStruct((48, 768), BF16)] * 4,
        in_specs=[SMEM, VMEM, VMEM],
        out_specs=[VMEM] * 8,
        scratch_shapes=[pltpu.VMEM((4, 96, 384), BF16), pltpu.VMEM((4, 48, 768), BF16)],
        compiler_params=pltpu.CompilerParams(vmem_limit_bytes=32 << 20),
    )(place, eig, sol)


def gather_kernel(*refs):
    blocks, out = refs[:4], refs[4]
    for r in range(2):
        for s in range(4):
            at = r * 384 + s * 96
            out[r * 4 + s] = jnp.concatenate([b[:, at : at + 96] for b in blocks], axis=1)


def gather_plane(blocks):
    return pl.pallas_call(
        gather_kernel,
        out_shape=jax.ShapeDtypeStruct((8, 48, 384), BF16),
        in_specs=[VMEM] * 4,
        out_specs=VMEM,
    )(*blocks)


def fields_kernel(place, col, sign_re, sign_im, *refs):
    sols = refs[:4]
    eig, cosine, sine, out, left, right, acc, fields, pairs = refs[4:]
    spot = place[1]
    lane = lax.broadcasted_iota(jnp.int32, (96, 384), 1)
    lane_n = lax.broadcasted_iota(jnp.int32, (32, 384), 1)
    for k in range(4):
        sol = sols[k]
        for g in range(4):
            for s in range(4):
                at = g * 4 + s
                src_re = sol[col[at]].astype(F32)
                src_im = sol[4 + col[at]].astype(F32)
                row, lanes = g * 96, slice(s * 384, (s + 1) * 384)
                left[row : row + 48, lanes] = (
                    sign_re[at] * src_re - sign_im[at] * src_im
                ).astype(BF16)
                left[row + 48 : row + 96, lanes] = (
                    sign_re[at] * src_im + sign_im[at] * src_re
                ).astype(BF16)

        def device(m, carry, k=k):
            both = []
            for half in range(2):
                w = eig[spot ^ m, half, k].astype(F32)
                w192 = shift_lanes(w, 192)
                w96 = shift_lanes(w, 96)
                w288 = shift_lanes(w192, 96)
                for first, middle, last in ((w, w96, w192), (w192, w288, w)):
                    a = jnp.where(lane < 96, first, jnp.where(lane < 288, middle, last))
                    both.append((a.reshape(3, 32, 384), shift_lanes(a, 192).reshape(3, 32, 384)))
            at = pl.multiple_of((k * 4 + m) * 32, 32)
            cos_all, sin_all = cosine[pl.ds(at, 32), :], sine[pl.ds(at, 32), :]
            for q in range(4):
                c0, c1 = cos_all[:, 2 * q : 2 * q + 1], cos_all[:, 2 * q + 1 : 2 * q + 2]
                s0, s1 = sin_all[:, 2 * q : 2 * q + 1], sin_all[:, 2 * q + 1 : 2 * q + 2]
                odd = (lane_n % 192) >= 96
                c = jnp.where(odd, c1, c0)
                c = jnp.where(lane_n < 192, c, -c)[None]
                d = -jnp.where(odd, s1, s0)[None]
                for s in range(4):
                    a, b = both[s]
                    y = c * a + d * b
                    row = pl.multiple_of(s * 384 + m * 96, 96)
                    right[pl.ds(row, 96), q * 384 : (q + 1) * 384] = y.reshape(96, 384).astype(BF16)
            return carry

        lax.fori_loop(0, 4, device, 0)

        def columns(n, carry, k=k):
            at = pl.ds(pl.multiple_of(n * 256, 256), 256)
            part = jnp.dot(left[...], right[:, at], preferred_element_type=F32)
            if k == 0:
                acc[:, at] = part
            else:
                acc[:, at] += part
            return carry

        lax.fori_loop(0, 6, columns, 0)

    flip = jnp.where(lax.broadcasted_iota(jnp.int32, (48, 384), 1) < 192, -1.0, 1.0).astype(F32)
    for q in range(4):
        lanes = slice(q * 384, (q + 1) * 384)
        rows = []
        for g in range(4):
            row = g * 96
            f = acc[row : row + 48, lanes] + flip * shift_lanes(acc[row + 48 : row + 96, lanes], 192)
            rows.append(f)
            out[g * 4 + q, 0:48, :] = f.astype(BF16)
        turned = [flip * shift_lanes(f, 192) for f in rows]
        for g in range(4):
            for h in range(g, 4):
                re = jnp.sum(rows[g] * rows[h], axis=0, keepdims=True)
                at, mirror = (g * 4 + h) * 2, (h * 4 + g) * 2
                pairs[at : at + 1, lanes] = re
                if h > g:
                    im = jnp.sum(rows[g] * turned[h], axis=0, keepdims=True)
                    pairs[mirror : mirror + 1, lanes] = re
                    pairs[at + 1 : at + 2, lanes] = im
                    pairs[mirror + 1 : mirror + 2, lanes] = -im
                else:
                    pairs[at + 1 : at + 2, lanes] = jnp.zeros_like(re)
    lane_p = lax.broadcasted_iota(jnp.int32, (8, 1536), 1)
    mom = lax.broadcasted_iota(jnp.int32, (8, 1536), 0)
    select = (lane_p // 384 * 2 + lane_p % 192 // 96 == mom).astype(F32)
    total = lax.dot_general(
        select,
        pairs[...],
        (((1,), (1,)), ((), ())),
        precision=lax.Precision.HIGHEST,
        preferred_element_type=F32,
    )
    high = total.astype(BF16)
    low = (total - high.astype(F32)).astype(BF16)
    tail = jnp.concatenate([high, low, jnp.zeros((8, 320), BF16)], axis=1)
    for block in range(16):
        out[block, 48:56, :] = tail


def local_fields(place, col, sign_re, sign_im, sols, eig, cosine, sine):
    return pl.pallas_call(
        fields_kernel,
        out_shape=jax.ShapeDtypeStruct((16, 56, 384), BF16),
        in_specs=[SMEM] * 4 + [VMEM] * 7,
        out_specs=VMEM,
        scratch_shapes=[
            pltpu.VMEM((384, 1536), BF16),
            pltpu.VMEM((1536, 1536), BF16),
            pltpu.VMEM((384, 1536), F32),
            pltpu.VMEM((8, 128), F32),
            pltpu.VMEM((32, 1536), F32),
        ],
        compiler_params=pltpu.CompilerParams(vmem_limit_bytes=48 << 20),
    )(place, col, sign_re, sign_im, *sols, eig, cosine, sine)


def join_kernel(blocks, out):
    for spot in range(4):
        rows = slice(spot * 48, (spot + 1) * 48)
        got = [blocks[z * 4 + spot, 0:48, :].astype(F32) for z in range(4)]
        for r in range(2):
            for p in range(2):
                at = r * 192 + p * 96
                out[r, rows, p * 384 : (p + 1) * 384] = jnp.concatenate(
                    [g[:, at : at + 96] for g in got], axis=1
                )


def join_fields(blocks):
    return pl.pallas_call(
        join_kernel,
        out_shape=jax.ShapeDtypeStruct((2, 192, 768), F32),
        in_specs=[VMEM],
        out_specs=VMEM,
        compiler_params=pltpu.CompilerParams(vmem_limit_bytes=32 << 20),
    )(blocks)


def swap(x, axis, mask):
    return lax.ppermute(x, axis, [(i, i ^ mask) for i in range(lax.axis_size(axis))])


def fast_body(eigvecs, solutions, momenta, gammas):
    z, spot, half = lax.axis_index("z"), lax.axis_index("plane"), lax.axis_index("mode")
    vec_count = eigvecs.shape[3]
    place = jnp.stack([z, spot, half]).astype(jnp.int32)
    eig = eigvecs.transpose(0, 2, 1, 3).reshape(2, 384, 384)
    sol = solutions.transpose(0, 2, 1, 3).reshape(2, 384, 192)
    prepared = prepare(place, eig, sol)
    eig_own, sol_own = prepared[:4], prepared[4:]
    eig_planes = [eig_own[0]] + [swap(eig_own[k], "z", k) for k in range(1, 4)]
    sol_plane = gather_plane([sol_own[0]] + [swap(sol_own[k], "plane", k) for k in range(1, 4)])
    sols = [sol_plane] + [swap(sol_plane, "z", k) for k in range(1, 4)]
    eig_all = lax.all_gather(jnp.stack(eig_planes), ("plane", "mode")).reshape(4, 2, 4, 96, 384)

    table = gamma_table()
    col_table = jnp.asarray(np.argmax(np.abs(table), axis=2).astype(np.int32))
    value = table.sum(axis=2)
    select = (gammas[:, None] == jnp.arange(16, dtype=jnp.int32)[None, :])[:, :, None]
    col = jnp.sum(jnp.where(select, col_table[None], 0), axis=1).reshape(16)
    sign_re = jnp.sum(jnp.where(select, jnp.asarray(value.real, F32)[None], 0.0), axis=1).reshape(16)
    sign_im = jnp.sum(jnp.where(select, jnp.asarray(value.imag, F32)[None], 0.0), axis=1).reshape(16)

    device = (z * 4 + spot) ^ jnp.arange(16, dtype=jnp.int32)
    site = (device[:, None] * 32 + jnp.arange(32, dtype=jnp.int32)[None, :]).reshape(512)
    coord_x, coord_y, coord_z = site // (LATT * LATT), site // LATT % LATT, site % LATT
    phase_int = (
        coord_x[:, None] * momenta[None, :, 0]
        + coord_y[:, None] * momenta[None, :, 1]
        + coord_z[:, None] * momenta[None, :, 2]
    ) % LATT
    theta = 2.0 * math.pi / LATT * phase_int.astype(F32)

    sent = local_fields(
        place, col, sign_re, sign_im, sols, eig_all, jnp.cos(theta), jnp.sin(theta)
    )
    got = lax.all_to_all(sent, ("z", "plane"), 0, 0, tiled=True)
    part = jnp.sum(got[:, 48:, :64].astype(F32), axis=0)
    part = part[:, :32] + part[:, 32:]
    part = part + swap(part, "mode", 1)
    traces = (part / float(vec_count * vec_count)).reshape(8, 4, 4, 2).transpose(1, 2, 0, 3)
    fields = join_fields(got).transpose(2, 0, 1)
    return fields, traces


def shifted(x, axis, by):
    count = lax.axis_size(axis)
    return lax.ppermute(x, axis, [(i, (i + by) % count) for i in range(count)])


def select_gammas(gammas):
    table = gamma_table()
    table_re, table_im = table.real.astype(np.float32), table.imag.astype(np.float32)
    select = (gammas[:, None] == jnp.arange(16, dtype=jnp.int32)[None, :]).astype(jnp.float32)
    count = gammas.shape[0]
    real_part = jnp.dot(
        select, jnp.asarray(table_re).reshape(16, 16), precision=lax.Precision.HIGHEST
    ).reshape(count, 4, 4)
    imag_part = jnp.dot(
        select, jnp.asarray(table_im).reshape(16, 16), precision=lax.Precision.HIGHEST
    ).reshape(count, 4, 4)
    return (real_part, imag_part)


def phases(momenta, first_site, count):
    index = first_site + jnp.arange(count, dtype=jnp.int32)
    coord_x = index // (LATT * LATT)
    coord_y = index // LATT % LATT
    coord_z = index % LATT
    phase_int = (
        momenta[:, 0:1] * coord_x[None, :]
        + momenta[:, 1:2] * coord_y[None, :]
        + momenta[:, 2:3] * coord_z[None, :]
    ) % LATT
    theta = 2.0 * math.pi / LATT * phase_int.astype(jnp.float32)
    return (jnp.cos(theta), jnp.sin(theta))


def left_side(vectors, cosine, sine_part):
    vec_re = vectors[0].astype(jnp.float32)[None]
    vec_im = vectors[1].astype(jnp.float32)[None]
    cosine = cosine[:, :, None, None]
    sine_part = sine_part[:, :, None, None]
    left_re = cosine * vec_re - sine_part * vec_im
    left_im = -(sine_part * vec_re + cosine * vec_im)
    return jnp.stack([left_re, left_im], 1).astype(jnp.bfloat16)


def right_side(vectors, gamma_re, gamma_im):
    count = vectors.shape[1]
    width = vectors.shape[3]
    sol_re = vectors[0].astype(jnp.float32).reshape(count, 4, 3, width)
    sol_im = vectors[1].astype(jnp.float32).reshape(count, 4, 3, width)
    high = lax.Precision.HIGHEST
    rot_re = jnp.einsum("gst,xtcj->gxscj", gamma_re, sol_re, precision=high) - jnp.einsum(
        "gst,xtcj->gxscj", gamma_im, sol_im, precision=high
    )
    rot_im = jnp.einsum("gst,xtcj->gxscj", gamma_re, sol_im, precision=high) + jnp.einsum(
        "gst,xtcj->gxscj", gamma_im, sol_re, precision=high
    )
    groups = gamma_re.shape[0]
    rot_re = rot_re.reshape(groups, count, 12, width)
    rot_im = rot_im.reshape(groups, count, 12, width)
    upper = jnp.stack([rot_re, rot_im], 3)
    lower = jnp.stack([-rot_im, rot_re], 3)
    return jnp.stack([upper, lower], 1).astype(jnp.bfloat16)


def general_body(eigvecs, solutions, momenta, gammas):
    local_sites = eigvecs.shape[1]
    vec_count = eigvecs.shape[3]
    col_count = solutions.shape[3]
    groups = gammas.shape[0]
    mom_count = momenta.shape[0]
    device = lax.axis_index("space")
    space_count = lax.axis_size("space")
    gamma_re, gamma_im = select_gammas(gammas)
    cosine, sine_part = phases(momenta, device * local_sites, local_sites)
    left = left_side(eigvecs, cosine, sine_part)
    right = right_side(solutions, gamma_re, gamma_im)
    partial_fields = jnp.einsum(
        "paxci,gaxcrj->gpirj", left, right, preferred_element_type=jnp.float32
    )
    partial_fields = partial_fields.reshape(groups * mom_count * vec_count, 2, col_count)
    fields = lax.psum_scatter(partial_fields, "space", scatter_dimension=0, tiled=True)
    own_rows = fields.shape[0]
    spacing = space_count // groups
    own_gamma = device // spacing
    row_index = device * own_rows + jnp.arange(own_rows, dtype=jnp.int32)
    row_mom = row_index % (mom_count * vec_count) // vec_count
    mom_onehot = (row_mom[:, None] == jnp.arange(mom_count, dtype=jnp.int32)[None, :]).astype(
        jnp.float32
    )
    gamma_range = jnp.arange(groups, dtype=jnp.int32)

    def pair_terms(first_rows, second_rows):
        real_sum = jnp.sum(
            first_rows[:, 0] * second_rows[:, 0] + first_rows[:, 1] * second_rows[:, 1], -1
        )
        imag_sum = jnp.sum(
            first_rows[:, 1] * second_rows[:, 0] - first_rows[:, 0] * second_rows[:, 1], -1
        )
        return jnp.dot(
            mom_onehot.T, jnp.stack([real_sum, imag_sum], 1), precision=lax.Precision.HIGHEST
        )

    def place(row_gamma, col_gamma, values):
        row_hot = (gamma_range == row_gamma).astype(jnp.float32)
        col_hot = (gamma_range == col_gamma).astype(jnp.float32)
        return row_hot[:, None, None, None] * col_hot[None, :, None, None] * values[None, None]

    total = place(own_gamma, own_gamma, pair_terms(fields, fields))
    last_shift = groups - 1
    for step in range(1, last_shift + 1):
        other = shifted(fields.astype(jnp.bfloat16), "space", step * spacing).astype(fields.dtype)
        values = pair_terms(fields, other)
        other_gamma = (own_gamma - step) % groups
        total = total + place(own_gamma, other_gamma, values)
    traces = lax.psum(total, ("space", "mode")) / float(vec_count * vec_count)
    return (fields, traces)


def solution(mesh):
    fits = dict(mesh.shape) == {"space": 16, "mode": 2}
    if fits:
        cut = Mesh(mesh.devices.reshape(4, 4, 2), ("z", "plane", "mode"))
        space = ("z", "plane")
    else:
        cut, space = mesh, "space"

    def step(eigvecs, solutions, momenta, gammas):
        sized = eigvecs.shape == (2, 512, 12, 384) and solutions.shape == (2, 512, 12, 384)
        sized = sized and momenta.shape == (8, 3) and gammas.shape == (4,)
        return jax.shard_map(
            fast_body if fits and sized else general_body,
            mesh=cut if fits and sized else mesh,
            in_specs=(
                P(None, space if fits and sized else "space", None, None),
                P(None, space if fits and sized else "space", None, "mode"),
                P(),
                P(),
            ),
            out_specs=(P(space if fits and sized else "space", None, "mode"), P()),
            check_vma=False,
        )(eigvecs, solutions, momenta, gammas)

    return step
```

```python
import functools
import math

import jax
import jax.numpy as jnp
import numpy as np
from jax import lax
from jax.experimental import pallas as pl
from jax.experimental.pallas import tpu as pltpu
from jax.sharding import Mesh
from jax.sharding import PartitionSpec as P

LATT = 96
VMEM = pl.BlockSpec(memory_space=pltpu.VMEM)
SMEM = pl.BlockSpec(memory_space=pltpu.SMEM)
BF16 = jnp.bfloat16
F32 = jnp.float32


def gamma_table():
    unit = 1j
    first = np.array([[0, 0, 0, unit], [0, 0, unit, 0], [0, -unit, 0, 0], [-unit, 0, 0, 0]])
    second = np.array([[0, 0, 0, -1], [0, 0, 1, 0], [0, 1, 0, 0], [-1, 0, 0, 0]], dtype=complex)
    third = np.array([[0, 0, unit, 0], [0, 0, 0, -unit], [-unit, 0, 0, 0], [0, unit, 0, 0]])
    fourth = np.array([[0, 0, 1, 0], [0, 0, 0, 1], [1, 0, 0, 0], [0, 1, 0, 0]], dtype=complex)
    basis = [first, second, third, fourth]
    table = []
    for number in range(16):
        matrix = np.eye(4, dtype=complex)
        for bit_pos in range(4):
            if number >> bit_pos & 1:
                matrix = matrix @ basis[bit_pos]
        table.append(matrix)
    return np.stack(table)


def shift_lanes(x, by):
    by = by % x.shape[-1]
    return x if by == 0 else pltpu.roll(x, by, x.ndim - 1)


def by_quarter(lane, first, second, third, fourth):
    return jnp.where(
        lane < 192, jnp.where(lane < 96, first, second), jnp.where(lane < 288, third, fourth)
    )


def prepare_kernel(place, eig, sol, *rest):
    eig_out, sol_out = rest[:4], rest[4:8]
    packs, turned = rest[8:]
    z, spot, half = place[0], place[1], place[2]
    start = pl.multiple_of(half * 192, 192)
    parts = [
        eig[0, pl.ds(start, 96), :].astype(F32),
        eig[1, pl.ds(start, 96), :].astype(F32),
        eig[0, pl.ds(start + 96, 96), :].astype(F32),
        eig[1, pl.ds(start + 96, 96), :].astype(F32),
    ]
    lane = lax.broadcasted_iota(jnp.int32, (96, 384), 1)
    for quarter in range(4):
        moved = [shift_lanes(part, 96 * (k - quarter)) for k, part in enumerate(parts)]
        packs[quarter] = by_quarter(lane, *moved).astype(BF16)
    for k in range(4):
        eig_out[k][...] = packs[z ^ k]
    for r in range(2):
        flipped = sol[r].astype(F32).T.astype(BF16)
        for k in range(4):
            turned[k, :, r * 384 : (r + 1) * 384] = flipped[k * 48 : (k + 1) * 48]
    for k in range(4):
        sol_out[k][...] = turned[spot ^ k]


def prepare(place, eig, sol):
    return pl.pallas_call(
        prepare_kernel,
        out_shape=[jax.ShapeDtypeStruct((96, 384), BF16)] * 4
        + [jax.ShapeDtypeStruct((48, 768), BF16)] * 4,
        in_specs=[SMEM, VMEM, VMEM],
        out_specs=[VMEM] * 8,
        scratch_shapes=[pltpu.VMEM((4, 96, 384), BF16), pltpu.VMEM((4, 48, 768), BF16)],
        compiler_params=pltpu.CompilerParams(vmem_limit_bytes=32 << 20),
    )(place, eig, sol)


def gather_kernel(*refs):
    blocks, out = refs[:4], refs[4]
    lane = lax.broadcasted_iota(jnp.int32, (48, 384), 1)
    for r in range(2):
        parts = [b[:, r * 384 : (r + 1) * 384].astype(F32) for b in blocks]
        for s in range(4):
            moved = [shift_lanes(part, 96 * (m - s)) for m, part in enumerate(parts)]
            out[r * 4 + s] = by_quarter(lane, *moved).astype(BF16)


def gather_plane(blocks):
    return pl.pallas_call(
        gather_kernel,
        out_shape=jax.ShapeDtypeStruct((8, 48, 384), BF16),
        in_specs=[VMEM] * 4,
        out_specs=VMEM,
    )(*blocks)


def build_left(sol, col, sign_re, sign_im, left):
    for g in range(4):
        for s in range(4):
            at = g * 4 + s
            src_re = sol[col[at]].astype(F32)
            src_im = sol[4 + col[at]].astype(F32)
            row, lanes = g * 96, slice(s * 384, (s + 1) * 384)
            left[row : row + 48, lanes] = (sign_re[at] * src_re - sign_im[at] * src_im).astype(BF16)
            left[row + 48 : row + 96, lanes] = (
                sign_re[at] * src_im + sign_im[at] * src_re
            ).astype(BF16)


def build_right(half, eigs, k, cosine, sine, right, m):
    lane = lax.broadcasted_iota(jnp.int32, (96, 384), 1)
    lane_n = lax.broadcasted_iota(jnp.int32, (32, 384), 1)
    both = []
    for other in range(2):
        w = eigs[m * 2 + other][k].astype(F32)
        w192 = shift_lanes(w, 192)
        w96 = shift_lanes(w, 96)
        w288 = shift_lanes(w192, 96)
        for low, (first, middle, last) in enumerate(((w, w96, w192), (w192, w288, w))):
            a = jnp.where(lane < 96, first, jnp.where(lane < 288, middle, last))
            row = pl.multiple_of(((half ^ other) * 2 + low) * 384 + m * 96, 96)
            both.append((row, a.reshape(3, 32, 384), shift_lanes(a, 192).reshape(3, 32, 384)))
    at = (k * 4 + m) * 32
    cos_all, sin_all = cosine[at : at + 32, :], sine[at : at + 32, :]
    odd = (lane_n % 192) >= 96
    for q in range(4):
        c0, c1 = cos_all[:, 2 * q : 2 * q + 1], cos_all[:, 2 * q + 1 : 2 * q + 2]
        s0, s1 = sin_all[:, 2 * q : 2 * q + 1], sin_all[:, 2 * q + 1 : 2 * q + 2]
        c = jnp.where(odd, c1, c0)
        c = jnp.where(lane_n < 192, c, -c)[None]
        d = -jnp.where(odd, s1, s0)[None]
        for row, a, b in both:
            y = c * a + d * b
            right[pl.ds(row, 96), q * 384 : (q + 1) * 384] = y.reshape(96, 384).astype(BF16)


def multiply(left, right, acc, first, n):
    at = slice(n * 256, (n + 1) * 256)
    part = jnp.dot(left[...], right[:, at], preferred_element_type=F32)
    if first:
        acc[:, at] = part
    else:
        acc[:, at] += part


def two_planes(place, col, sign_re, sign_im, sols, eigs, planes, tables, lefts, rights, acc, first):
    half = place[2]
    cosine, sine = tables
    for m in range(4):
        build_right(half, eigs, planes[0], cosine, sine, rights[0], m)
    build_left(sols[0], col, sign_re, sign_im, lefts[0])
    for n in range(6):
        multiply(lefts[0], rights[0], acc, first, n)
        if n < 4:
            build_right(half, eigs, planes[1], cosine, sine, rights[1], n)
        if n == 4:
            build_left(sols[1], col, sign_re, sign_im, lefts[1])
    for n in range(6):
        multiply(lefts[1], rights[1], acc, False, n)


def first_kernel(place, col, sign_re, sign_im, *refs):
    sols, eigs, tables, acc = refs[:2], refs[2:10], refs[10:12], refs[12]
    lefts, rights = refs[13:15], refs[15:17]
    two_planes(place, col, sign_re, sign_im, sols, eigs, (0, 1), tables, lefts, rights, acc, True)


def last_kernel(place, col, sign_re, sign_im, *refs):
    sols, eigs, tables, acc_in, out = refs[:2], refs[2:10], refs[10:12], refs[12], refs[13]
    lefts, rights, acc, pairs = refs[14:16], refs[16:18], refs[18], refs[19]
    acc[...] = acc_in[...]
    two_planes(place, col, sign_re, sign_im, sols, eigs, (2, 3), tables, lefts, rights, acc, False)
    flip = jnp.where(lax.broadcasted_iota(jnp.int32, (48, 384), 1) < 192, -1.0, 1.0).astype(F32)
    for q in range(4):
        lanes = slice(q * 384, (q + 1) * 384)
        rows = []
        for g in range(4):
            row = g * 96
            f = acc[row : row + 48, lanes] + flip * shift_lanes(acc[row + 48 : row + 96, lanes], 192)
            rows.append(f)
            out[g * 4 + q, 0:48, :] = f.astype(BF16)
        turned = [flip * shift_lanes(f, 192) for f in rows]
        for g in range(4):
            for h in range(g, 4):
                re = jnp.sum(rows[g] * rows[h], axis=0, keepdims=True)
                at, mirror = (g * 4 + h) * 2, (h * 4 + g) * 2
                pairs[at : at + 1, lanes] = re
                if h > g:
                    im = jnp.sum(rows[g] * turned[h], axis=0, keepdims=True)
                    pairs[mirror : mirror + 1, lanes] = re
                    pairs[at + 1 : at + 2, lanes] = im
                    pairs[mirror + 1 : mirror + 2, lanes] = -im
                else:
                    pairs[at + 1 : at + 2, lanes] = jnp.zeros_like(re)
    lane_p = lax.broadcasted_iota(jnp.int32, (8, 1536), 1)
    mom = lax.broadcasted_iota(jnp.int32, (8, 1536), 0)
    select = (lane_p // 384 * 2 + lane_p % 192 // 96 == mom).astype(F32)
    total = lax.dot_general(
        select,
        pairs[...],
        (((1,), (1,)), ((), ())),
        precision=lax.Precision.HIGHEST,
        preferred_element_type=F32,
    )
    high = total.astype(BF16)
    low = (total - high.astype(F32)).astype(BF16)
    tail = jnp.concatenate([high, low, jnp.zeros((8, 320), BF16)], axis=1)
    for block in range(16):
        out[block, 48:56, :] = tail


WORK = [pltpu.VMEM((384, 1536), BF16)] * 2 + [pltpu.VMEM((1536, 1536), BF16)] * 2


def first_planes(scalars, sols, eigs, tables):
    return pl.pallas_call(
        first_kernel,
        out_shape=jax.ShapeDtypeStruct((384, 1536), F32),
        in_specs=[SMEM] * 4 + [VMEM] * 12,
        out_specs=VMEM,
        scratch_shapes=WORK,
        compiler_params=pltpu.CompilerParams(vmem_limit_bytes=40 << 20),
    )(*scalars, *sols, *eigs, *tables)


def last_planes(scalars, sols, eigs, tables, acc):
    return pl.pallas_call(
        last_kernel,
        out_shape=jax.ShapeDtypeStruct((16, 56, 384), BF16),
        in_specs=[SMEM] * 4 + [VMEM] * 13,
        out_specs=VMEM,
        scratch_shapes=WORK + [pltpu.VMEM((384, 1536), F32), pltpu.VMEM((32, 1536), F32)],
        compiler_params=pltpu.CompilerParams(vmem_limit_bytes=40 << 20),
    )(*scalars, *sols, *eigs, *tables, acc)


def join_kernel(blocks, out):
    for spot in range(4):
        rows = slice(spot * 48, (spot + 1) * 48)
        got = [blocks[z * 4 + spot, 0:48, :].astype(F32) for z in range(4)]
        for r in range(2):
            for p in range(2):
                at = r * 192 + p * 96
                out[r, rows, p * 384 : (p + 1) * 384] = jnp.concatenate(
                    [g[:, at : at + 96] for g in got], axis=1
                )


def join_fields(blocks):
    return pl.pallas_call(
        join_kernel,
        out_shape=jax.ShapeDtypeStruct((2, 192, 768), F32),
        in_specs=[VMEM],
        out_specs=VMEM,
        compiler_params=pltpu.CompilerParams(vmem_limit_bytes=32 << 20),
    )(blocks)


def swap(x, axis, mask):
    return lax.ppermute(x, axis, [(i, i ^ mask) for i in range(lax.axis_size(axis))])


def swap_both(x):
    pairs = [(i * 2 + y, (i ^ 2) * 2 + (y ^ 1)) for i in range(4) for y in range(2)]
    return lax.ppermute(x, ("plane", "mode"), pairs)


def fast_body(eigvecs, solutions, momenta, gammas):
    z, spot, half = lax.axis_index("z"), lax.axis_index("plane"), lax.axis_index("mode")
    vec_count = eigvecs.shape[3]
    place = jnp.stack([z, spot, half]).astype(jnp.int32)
    eig = eigvecs.transpose(0, 2, 1, 3).reshape(2, 384, 384)
    sol = solutions.transpose(0, 2, 1, 3).reshape(2, 384, 192)
    prepared = prepare(place, eig, sol)
    eig_own, sol_own = prepared[:4], prepared[4:]
    eig_planes = [eig_own[0]] + [swap(eig_own[k], "z", k) for k in range(1, 4)]
    sol_plane = gather_plane([sol_own[0]] + [swap(sol_own[k], "plane", k) for k in range(1, 4)])
    sols = [sol_plane] + [swap(sol_plane, "z", k) for k in range(1, 4)]
    mine = jnp.stack(eig_planes)
    chip = [mine, swap(mine, "mode", 1), swap(mine, "plane", 2)]
    chip.append(swap_both(mine))
    core = [swap(block, "plane", 1) for block in chip]
    eigs = [chip[0], chip[1], core[0], core[1], chip[2], chip[3], core[2], core[3]]

    table = gamma_table()
    col_table = jnp.asarray(np.argmax(np.abs(table), axis=2).astype(np.int32))
    value = table.sum(axis=2)
    select = (gammas[:, None] == jnp.arange(16, dtype=jnp.int32)[None, :])[:, :, None]
    col = jnp.sum(jnp.where(select, col_table[None], 0), axis=1).reshape(16)
    sign_re = jnp.sum(jnp.where(select, jnp.asarray(value.real, F32)[None], 0.0), axis=1).reshape(16)
    sign_im = jnp.sum(jnp.where(select, jnp.asarray(value.imag, F32)[None], 0.0), axis=1).reshape(16)

    device = (z * 4 + spot) ^ jnp.arange(16, dtype=jnp.int32)
    site = (device[:, None] * 32 + jnp.arange(32, dtype=jnp.int32)[None, :]).reshape(512)
    coord_x, coord_y, coord_z = site // (LATT * LATT), site // LATT % LATT, site % LATT
    phase_int = (
        coord_x[:, None] * momenta[None, :, 0]
        + coord_y[:, None] * momenta[None, :, 1]
        + coord_z[:, None] * momenta[None, :, 2]
    ) % LATT
    theta = 2.0 * math.pi / LATT * phase_int.astype(F32)

    scalars, tables = (place, col, sign_re, sign_im), (jnp.cos(theta), jnp.sin(theta))
    acc = first_planes(scalars, sols[:2], eigs, tables)
    sent = last_planes(scalars, sols[2:], eigs, tables, acc)
    got = lax.all_to_all(sent, ("z", "plane"), 0, 0, tiled=True)
    part = jnp.sum(got[:, 48:, :64].astype(F32), axis=0)
    part = part[:, :32] + part[:, 32:]
    part = part + swap(part, "mode", 1)
    traces = (part / float(vec_count * vec_count)).reshape(8, 4, 4, 2).transpose(1, 2, 0, 3)
    fields = join_fields(got).transpose(2, 0, 1)
    return fields, traces


def shifted(x, axis, by):
    count = lax.axis_size(axis)
    return lax.ppermute(x, axis, [(i, (i + by) % count) for i in range(count)])


def select_gammas(gammas):
    table = gamma_table()
    table_re, table_im = table.real.astype(np.float32), table.imag.astype(np.float32)
    select = (gammas[:, None] == jnp.arange(16, dtype=jnp.int32)[None, :]).astype(jnp.float32)
    count = gammas.shape[0]
    real_part = jnp.dot(
        select, jnp.asarray(table_re).reshape(16, 16), precision=lax.Precision.HIGHEST
    ).reshape(count, 4, 4)
    imag_part = jnp.dot(
        select, jnp.asarray(table_im).reshape(16, 16), precision=lax.Precision.HIGHEST
    ).reshape(count, 4, 4)
    return (real_part, imag_part)


def phases(momenta, first_site, count):
    index = first_site + jnp.arange(count, dtype=jnp.int32)
    coord_x = index // (LATT * LATT)
    coord_y = index // LATT % LATT
    coord_z = index % LATT
    phase_int = (
        momenta[:, 0:1] * coord_x[None, :]
        + momenta[:, 1:2] * coord_y[None, :]
        + momenta[:, 2:3] * coord_z[None, :]
    ) % LATT
    theta = 2.0 * math.pi / LATT * phase_int.astype(jnp.float32)
    return (jnp.cos(theta), jnp.sin(theta))


def left_side(vectors, cosine, sine_part):
    vec_re = vectors[0].astype(jnp.float32)[None]
    vec_im = vectors[1].astype(jnp.float32)[None]
    cosine = cosine[:, :, None, None]
    sine_part = sine_part[:, :, None, None]
    left_re = cosine * vec_re - sine_part * vec_im
    left_im = -(sine_part * vec_re + cosine * vec_im)
    return jnp.stack([left_re, left_im], 1).astype(jnp.bfloat16)


def right_side(vectors, gamma_re, gamma_im):
    count = vectors.shape[1]
    width = vectors.shape[3]
    sol_re = vectors[0].astype(jnp.float32).reshape(count, 4, 3, width)
    sol_im = vectors[1].astype(jnp.float32).reshape(count, 4, 3, width)
    high = lax.Precision.HIGHEST
    rot_re = jnp.einsum("gst,xtcj->gxscj", gamma_re, sol_re, precision=high) - jnp.einsum(
        "gst,xtcj->gxscj", gamma_im, sol_im, precision=high
    )
    rot_im = jnp.einsum("gst,xtcj->gxscj", gamma_re, sol_im, precision=high) + jnp.einsum(
        "gst,xtcj->gxscj", gamma_im, sol_re, precision=high
    )
    groups = gamma_re.shape[0]
    rot_re = rot_re.reshape(groups, count, 12, width)
    rot_im = rot_im.reshape(groups, count, 12, width)
    upper = jnp.stack([rot_re, rot_im], 3)
    lower = jnp.stack([-rot_im, rot_re], 3)
    return jnp.stack([upper, lower], 1).astype(jnp.bfloat16)


def general_body(eigvecs, solutions, momenta, gammas):
    local_sites = eigvecs.shape[1]
    vec_count = eigvecs.shape[3]
    col_count = solutions.shape[3]
    groups = gammas.shape[0]
    mom_count = momenta.shape[0]
    device = lax.axis_index("space")
    space_count = lax.axis_size("space")
    gamma_re, gamma_im = select_gammas(gammas)
    cosine, sine_part = phases(momenta, device * local_sites, local_sites)
    left = left_side(eigvecs, cosine, sine_part)
    right = right_side(solutions, gamma_re, gamma_im)
    partial_fields = jnp.einsum(
        "paxci,gaxcrj->gpirj", left, right, preferred_element_type=jnp.float32
    )
    partial_fields = partial_fields.reshape(groups * mom_count * vec_count, 2, col_count)
    fields = lax.psum_scatter(partial_fields, "space", scatter_dimension=0, tiled=True)
    own_rows = fields.shape[0]
    spacing = space_count // groups
    own_gamma = device // spacing
    row_index = device * own_rows + jnp.arange(own_rows, dtype=jnp.int32)
    row_mom = row_index % (mom_count * vec_count) // vec_count
    mom_onehot = (row_mom[:, None] == jnp.arange(mom_count, dtype=jnp.int32)[None, :]).astype(
        jnp.float32
    )
    gamma_range = jnp.arange(groups, dtype=jnp.int32)

    def pair_terms(first_rows, second_rows):
        real_sum = jnp.sum(
            first_rows[:, 0] * second_rows[:, 0] + first_rows[:, 1] * second_rows[:, 1], -1
        )
        imag_sum = jnp.sum(
            first_rows[:, 1] * second_rows[:, 0] - first_rows[:, 0] * second_rows[:, 1], -1
        )
        return jnp.dot(
            mom_onehot.T, jnp.stack([real_sum, imag_sum], 1), precision=lax.Precision.HIGHEST
        )

    def place(row_gamma, col_gamma, values):
        row_hot = (gamma_range == row_gamma).astype(jnp.float32)
        col_hot = (gamma_range == col_gamma).astype(jnp.float32)
        return row_hot[:, None, None, None] * col_hot[None, :, None, None] * values[None, None]

    total = place(own_gamma, own_gamma, pair_terms(fields, fields))
    last_shift = groups - 1
    for step in range(1, last_shift + 1):
        other = shifted(fields.astype(jnp.bfloat16), "space", step * spacing).astype(fields.dtype)
        values = pair_terms(fields, other)
        other_gamma = (own_gamma - step) % groups
        total = total + place(own_gamma, other_gamma, values)
    traces = lax.psum(total, ("space", "mode")) / float(vec_count * vec_count)
    return (fields, traces)


def solution(mesh):
    fits = dict(mesh.shape) == {"space": 16, "mode": 2}
    if fits:
        cut = Mesh(mesh.devices.reshape(4, 4, 2), ("z", "plane", "mode"))
        space = ("z", "plane")
    else:
        cut, space = mesh, "space"

    def step(eigvecs, solutions, momenta, gammas):
        sized = eigvecs.shape == (2, 512, 12, 384) and solutions.shape == (2, 512, 12, 384)
        sized = sized and momenta.shape == (8, 3) and gammas.shape == (4,)
        return jax.shard_map(
            fast_body if fits and sized else general_body,
            mesh=cut if fits and sized else mesh,
            in_specs=(
                P(None, space if fits and sized else "space", None, None),
                P(None, space if fits and sized else "space", None, "mode"),
                P(),
                P(),
            ),
            out_specs=(P(space if fits and sized else "space", None, "mode"), P()),
            check_vma=False,
        )(eigvecs, solutions, momenta, gammas)

    return step
```

```python
import functools
import math

import jax
import jax.numpy as jnp
import numpy as np
from jax import lax
from jax.experimental import pallas as pl
from jax.experimental.pallas import tpu as pltpu
from jax.sharding import Mesh
from jax.sharding import PartitionSpec as P

LATT = 96
VMEM = pl.BlockSpec(memory_space=pltpu.VMEM)
SMEM = pl.BlockSpec(memory_space=pltpu.SMEM)
HBM = pl.BlockSpec(memory_space=pltpu.HBM)
BF16 = jnp.bfloat16
F32 = jnp.float32


def gamma_table():
    unit = 1j
    first = np.array([[0, 0, 0, unit], [0, 0, unit, 0], [0, -unit, 0, 0], [-unit, 0, 0, 0]])
    second = np.array([[0, 0, 0, -1], [0, 0, 1, 0], [0, 1, 0, 0], [-1, 0, 0, 0]], dtype=complex)
    third = np.array([[0, 0, unit, 0], [0, 0, 0, -unit], [-unit, 0, 0, 0], [0, unit, 0, 0]])
    fourth = np.array([[0, 0, 1, 0], [0, 0, 0, 1], [1, 0, 0, 0], [0, 1, 0, 0]], dtype=complex)
    basis = [first, second, third, fourth]
    table = []
    for number in range(16):
        matrix = np.eye(4, dtype=complex)
        for bit_pos in range(4):
            if number >> bit_pos & 1:
                matrix = matrix @ basis[bit_pos]
        table.append(matrix)
    return np.stack(table)


def shift_lanes(x, by):
    by = by % x.shape[-1]
    return x if by == 0 else pltpu.roll(x, by, x.ndim - 1)


def by_quarter(lane, first, second, third, fourth):
    tiles = []
    for k, (low, high) in enumerate(((first, second), (second, third), (third, fourth))):
        at = slice(k * 128, (k + 1) * 128)
        tiles.append(jnp.where(lane[:, at] < (k + 1) * 96, wide(low, at), wide(high, at)))
    return jnp.concatenate(tiles, axis=1)


def wide(x, at):
    return x[:, at] if x.shape[1] > 1 else x


def here():
    return lax.axis_index("z"), lax.axis_index("x"), lax.axis_index("core")


def prepare_sol_kernel(sol, sol_own, sol_other, turned):
    x = lax.axis_index("x")
    for r in range(2):
        flipped = sol[r].astype(F32).T.astype(BF16)
        for k in range(2):
            turned[k, :, r * 384 : (r + 1) * 384] = flipped[k * 96 : (k + 1) * 96]
    sol_own[...] = turned[x]
    sol_other[...] = turned[x ^ 1]


def prepare_sol(sol):
    return pl.pallas_call(
        prepare_sol_kernel,
        out_shape=[jax.ShapeDtypeStruct((96, 768), BF16)] * 2,
        in_specs=[VMEM],
        out_specs=[VMEM] * 2,
        scratch_shapes=[pltpu.VMEM((2, 96, 768), BF16)],
        compiler_params=pltpu.CompilerParams(vmem_limit_bytes=16 << 20),
    )(sol)


def prepare_eig_kernel(momenta, eig, after, full, *rest):
    eig_out, (cosine, sine, packs) = rest[:3], rest[3:]
    (z, x, core), half = here(), lax.axis_index("mode")
    lane = lax.broadcasted_iota(jnp.int32, (96, 384), 1)
    for side in range(2):
        at = side * 192
        parts = [
            eig[r, at + low * 96 : at + low * 96 + 96, :].astype(F32)
            for low in range(2)
            for r in range(2)
        ]
        for quarter in range(4):
            moved = [shift_lanes(part, 96 * (k - quarter)) for k, part in enumerate(parts)]
            packs[quarter, side] = by_quarter(lane, *moved).astype(BF16)
    full[0:96] = packs[z, 0]
    full[96:192] = packs[z, 1]
    for k in range(1, 4):
        eig_out[k - 1][...] = packs[z ^ k, half]
    shape = cosine.shape[::-1]
    mom = lax.broadcasted_iota(jnp.int32, shape, 0)
    lane = lax.broadcasted_iota(jnp.int32, shape, 1)
    device = (z * 4 + x * 2 + core) ^ ((lane >> 5) << 1)
    site = (device * 32 + (lane & 31)).astype(F32)
    line = jnp.floor((site + 0.5) * (1.0 / LATT))
    coord_x = jnp.floor((line + 0.5) * (1.0 / LATT))
    coords = (coord_x, line - LATT * coord_x, site - LATT * line)
    steps = jnp.zeros(shape, F32)
    for axis, coord in enumerate(coords):
        factor = jnp.zeros(shape, F32)
        for p in range(8):
            factor = jnp.where(mom == p, momenta[axis, p].astype(F32), factor)
        steps += factor * coord
    steps -= LATT * jnp.floor((steps + 0.5) * (1.0 / LATT))
    theta = 2.0 * math.pi / LATT * steps
    cosine[...] = jnp.cos(theta).T
    sine[...] = jnp.sin(theta).T


def prepare_eig(momenta, eig, after):
    return pl.pallas_call(
        prepare_eig_kernel,
        out_shape=[jax.ShapeDtypeStruct((192, 384), BF16)]
        + [jax.ShapeDtypeStruct((96, 384), BF16)] * 3
        + [jax.ShapeDtypeStruct((256, 8), F32)] * 2,
        in_specs=[SMEM, VMEM, HBM],
        out_specs=[VMEM] * 6,
        scratch_shapes=[pltpu.VMEM((4, 2, 96, 384), BF16)],
        compiler_params=pltpu.CompilerParams(vmem_limit_bytes=16 << 20),
    )(momenta, eig, after)


def build_base(first, second, base):
    lane = lax.broadcasted_iota(jnp.int32, (96, 384), 1)
    parts = [
        [plane[m, :, r * 384 : (r + 1) * 384].astype(F32) for plane in (first, second) for m in range(2)]
        for r in range(2)
    ]
    for t in range(4):
        re, im = [
            by_quarter(lane, *[shift_lanes(x, 96 * (k - t)) for k, x in enumerate(part)])
            for part in parts
        ]
        for turn, x in enumerate((re, -im, -re, im)):
            base[turn * 4 + t] = x.astype(BF16)


def build_left(base, gammas, table, left):
    for g in range(4):
        for part in range(2):
            at = g * 192 + part * 96
            for s in range(4):
                source = table[gammas[g] * 8 + part * 4 + s]
                left[at : at + 96, s * 384 : (s + 1) * 384] = base[source]


def build_phases(cosine, sine, at, phases):
    lane = lax.broadcasted_iota(jnp.int32, (32, 384), 1)
    for part, table in enumerate((cosine, sine)):
        rows = table[at : at + 32, :]
        for h in range(2):
            four = [rows[:, p : p + 1] for p in (2 * h, 2 * h + 1, 2 * h + 4, 2 * h + 5)]
            phases[h, part] = by_quarter(lane, *four)


def build_right(blocks, k, m, cosine, sine, right, phases, spread):
    lane = lax.broadcasted_iota(jnp.int32, (96, 384), 1)
    build_phases(cosine, sine, (k * 2 + m) * 32, phases)
    for side, (spin, block) in enumerate(blocks):
        w = block.astype(F32)
        turns = [shift_lanes(w, 96 * by) for by in range(4)]
        for part in range(4):
            x = by_quarter(lane, *[turns[(k4 - part) % 4] for k4 in range(4)])
            spread[side, part] = -x if part % 2 else x
    for h in range(2):
        cos, sin = phases[h, 0][None], phases[h, 1][None]
        for side, (spin, _) in enumerate(blocks):
            for low in range(2):
                re = spread[side, low * 2].reshape(3, 32, 384)
                im = spread[side, low * 2 + 1].reshape(3, 32, 384)
                at = (spin + low) * 384 + (k % 2) * 192 + m * 96
                rows = slice(at, at + 96)
                right[h, rows, 0:384] = (cos * re + sin * im).reshape(96, 384).astype(BF16)
                right[h, rows, 384:768] = (cos * im - sin * re).reshape(96, 384).astype(BF16)


def far_blocks(eigs, k, m):
    x = lax.axis_index("x")
    return [(half * 2, eigs[x ^ m, half, k - 1]) for half in range(2)]


def product(left, right, side, n):
    at = slice(n * 256, (n + 1) * 256)
    return at, jnp.dot(left[...], right[side, :, at], preferred_element_type=F32)


def near_kernel(gammas, table, *refs):
    sols, fulls, eigs, (cosine, sine) = refs[:2], refs[2:4], refs[4], refs[5:7]
    accs, far_right, (base, left, right, phases, spread) = refs[7:9], refs[9], refs[10:]
    work = (phases, spread)
    for m in range(2):
        blocks = [(0, fulls[m][0:96]), (2, fulls[m][96:192])]
        build_right(blocks, 0, m, cosine, sine, right, *work)
    build_base(*sols, base)
    build_left(base, gammas, table, left)
    for k in range(1, 4):
        for m in range(2):
            build_right(far_blocks(eigs, k, m), k, m, cosine, sine, far_right if k > 1 else right, *work)
    core = lax.axis_index("core")
    for acc, side in ((accs[0], core), (accs[1], core ^ 1)):
        for n in range(3):
            at, part = product(left, right, side, n)
            acc[:, at] = part


def given_kernel(gammas, table, first, second, right, acc, out, left, base):
    build_base(first, second, base)
    build_left(base, gammas, table, left)
    for n in range(3):
        at, part = product(left, right, lax.axis_index("core") ^ 1, n)
        out[:, at] = (acc[:, at] + part).astype(BF16)


def own_kernel(left, right, acc, out):
    for n in range(3):
        at, part = product(left, right, lax.axis_index("core"), n)
        out[:, at] = acc[:, at] + part


def finish_kernel(own, got, *rest):
    outs, pairs = rest[:8], rest[8]
    z, x, _ = here()
    low = lax.broadcasted_iota(jnp.int32, (96, 384), 1) < 192
    gs, res, ims = [z ^ k for k in range(4)], [], []
    for k in range(4):
        (a, b), (c, d) = [
            [
                own[pl.ds(at, 96), lanes] + got[pl.ds(at, 96), lanes].astype(F32)
                for lanes in (slice(0, 384), slice(384, 768))
            ]
            for at in (pl.multiple_of(gs[k] * 192, 96), pl.multiple_of(gs[k] * 192 + 96, 96))
        ]
        re, im = a - d, b + c
        res.append(re)
        ims.append(im)
        first = jnp.where(low, re, shift_lanes(im, 192))
        second = jnp.where(low, shift_lanes(re, 192), im)
        outs[k * 2][0:96] = jnp.where(x == 0, first, second).astype(BF16)
        outs[k * 2 + 1][0:96] = jnp.where(x == 0, second, first).astype(BF16)
    for i in range(4):
        for k in range(i, 4):
            at, mirror = (gs[i] * 4 + gs[k]) * 2, (gs[k] * 4 + gs[i]) * 2
            both = jnp.sum(res[i] * res[k] + ims[i] * ims[k], axis=0, keepdims=True)
            pairs[pl.ds(at, 1), :] = both
            if k > i:
                turn = jnp.sum(ims[i] * res[k] - res[i] * ims[k], axis=0, keepdims=True)
                pairs[pl.ds(mirror, 1), :] = both
                pairs[pl.ds(at + 1, 1), :] = turn
                pairs[pl.ds(mirror + 1, 1), :] = -turn
            else:
                pairs[pl.ds(at + 1, 1), :] = jnp.zeros_like(both)
    lane_p = lax.broadcasted_iota(jnp.int32, (8, 384), 1)
    mom = lax.broadcasted_iota(jnp.int32, (8, 384), 0)
    total = lax.dot_general(
        (lane_p // 96 == mom).astype(F32),
        pairs[...],
        (((1,), (1,)), ((), ())),
        precision=lax.Precision.HIGHEST,
        preferred_element_type=F32,
    )
    high = total.astype(BF16)
    low_part = (total - high.astype(F32)).astype(BF16)
    tail = jnp.concatenate([high, low_part, jnp.zeros((8, 320), BF16)], axis=1)
    for k in range(8):
        outs[k][96:104] = tail


BASE = pltpu.VMEM((16, 96, 384), BF16)
SPREAD = [pltpu.VMEM((2, 2, 32, 384), F32), pltpu.VMEM((2, 4, 96, 384), F32)]


def call(kernel, inputs, scalars, out_shape, scratch=(), limit=24):
    return pl.pallas_call(
        kernel,
        out_shape=out_shape,
        in_specs=[SMEM] * len(scalars) + [VMEM] * len(inputs),
        out_specs=jax.tree.map(lambda _: VMEM, out_shape),
        scratch_shapes=scratch,
        compiler_params=pltpu.CompilerParams(vmem_limit_bytes=limit << 20),
    )(*scalars, *inputs)


def join_kernel(*refs):
    got, out, blocks = refs[:8], refs[8], refs[9]
    z, x, _ = here()
    for k in range(8):
        blocks[(z ^ (k // 2)) * 2 + (x ^ (k % 2))] = got[k][0:96]
    for side in range(2):
        rows = slice(side * 96, (side + 1) * 96)
        parts = [blocks[k * 2 + side].astype(F32) for k in range(4)]
        for r in range(2):
            for p in range(2):
                at = r * 192 + p * 96
                out[r, rows, p * 384 : (p + 1) * 384] = jnp.concatenate(
                    [part[:, at : at + 96] for part in parts], axis=1
                )


def swap(x, axis, mask):
    return lax.ppermute(x, axis, [(i, i ^ mask) for i in range(lax.axis_size(axis))])


def fast_body(eigvecs, solutions, momenta, gammas):
    vec_count = eigvecs.shape[3]
    eig = eigvecs.transpose(0, 2, 1, 3).reshape(2, 384, 384)
    sol = solutions.transpose(0, 2, 1, 3).reshape(2, 384, 192)
    sol_own, sol_other = prepare_sol(sol)
    full, *eig_own, cosine, sine = prepare_eig(momenta.T, eig, sol_other)
    tables = (cosine, sine)
    sol_pair = jnp.stack([sol_own, swap(sol_other, "x", 1)])
    mine = jnp.stack([swap(eig_own[k - 1], "z", k) for k in range(1, 4)])
    sols = [sol_pair] + [swap(sol_pair, "z", k) for k in range(1, 4)]

    table = gamma_table()
    spin = np.argmax(np.abs(table), axis=2)
    turn = np.round(np.angle(table.sum(axis=2)) / (np.pi / 2)).astype(int) % 4
    rows = np.stack([turn * 4 + spin, (turn + 3) % 4 * 4 + spin], axis=1)
    scalars = (gammas, jnp.asarray(rows.astype(np.int32).reshape(128)))

    total = jax.ShapeDtypeStruct((768, 768), F32)
    left, right = pltpu.VMEM((768, 1536), BF16), (2, 1536, 768)
    eig_all = lax.all_gather(mine, ("x", "mode")).reshape(2, 2, 3, 96, 384)
    acc_own, acc_other, right = call(
        near_kernel,
        [*sols[:2], full, swap(full, "x", 1), eig_all, *tables],
        scalars,
        [total] * 2 + [jax.ShapeDtypeStruct(right, BF16)],
        [
            BASE,
            left,
            pltpu.VMEM(right, BF16),
            *SPREAD,
        ],
        36,
    )
    given, left = call(
        given_kernel,
        [*sols[2:], right, acc_other],
        scalars,
        [jax.ShapeDtypeStruct((768, 768), BF16), jax.ShapeDtypeStruct((768, 1536), BF16)],
        [BASE],
    )
    taken = swap(given, "core", 1)
    own = call(own_kernel, [left, right, acc_own], [], total)
    sent = call(
        finish_kernel,
        [own, taken],
        [],
        [jax.ShapeDtypeStruct((104, 384), BF16)] * 8,
        [pltpu.VMEM((32, 384), F32)],
    )
    got = [sent[0]] + [swap(sent[k], ("z", "x"), k) for k in range(1, 8)]
    part = sum(block[96:100, :64].astype(F32) for block in got)
    part = part[:, :32] + part[:, 32:]
    other = swap(part, "core", 1) + swap(part, ("core", "mode"), 3)
    part = part + swap(part, "mode", 1)
    first = lax.axis_index("core") == 0
    pair = jnp.stack([jnp.where(first, part, other), jnp.where(first, other, part)])
    traces = (pair / float(vec_count * vec_count)).reshape(2, 2, 2, 4, 4, 2)
    traces = traces.transpose(3, 4, 1, 0, 2, 5).reshape(4, 4, 8, 2)
    fields = call(
        join_kernel,
        got,
        [],
        jax.ShapeDtypeStruct((2, 192, 768), F32),
        [pltpu.VMEM((8, 96, 384), BF16)],
    ).transpose(2, 0, 1)
    return fields, traces


def shifted(x, axis, by):
    count = lax.axis_size(axis)
    return lax.ppermute(x, axis, [(i, (i + by) % count) for i in range(count)])


def select_gammas(gammas):
    table = gamma_table()
    table_re, table_im = table.real.astype(np.float32), table.imag.astype(np.float32)
    select = (gammas[:, None] == jnp.arange(16, dtype=jnp.int32)[None, :]).astype(jnp.float32)
    count = gammas.shape[0]
    real_part = jnp.dot(
        select, jnp.asarray(table_re).reshape(16, 16), precision=lax.Precision.HIGHEST
    ).reshape(count, 4, 4)
    imag_part = jnp.dot(
        select, jnp.asarray(table_im).reshape(16, 16), precision=lax.Precision.HIGHEST
    ).reshape(count, 4, 4)
    return (real_part, imag_part)


def phases(momenta, first_site, count):
    index = first_site + jnp.arange(count, dtype=jnp.int32)
    coord_x = index // (LATT * LATT)
    coord_y = index // LATT % LATT
    coord_z = index % LATT
    phase_int = (
        momenta[:, 0:1] * coord_x[None, :]
        + momenta[:, 1:2] * coord_y[None, :]
        + momenta[:, 2:3] * coord_z[None, :]
    ) % LATT
    theta = 2.0 * math.pi / LATT * phase_int.astype(jnp.float32)
    return (jnp.cos(theta), jnp.sin(theta))


def left_side(vectors, cosine, sine_part):
    vec_re = vectors[0].astype(jnp.float32)[None]
    vec_im = vectors[1].astype(jnp.float32)[None]
    cosine = cosine[:, :, None, None]
    sine_part = sine_part[:, :, None, None]
    left_re = cosine * vec_re - sine_part * vec_im
    left_im = -(sine_part * vec_re + cosine * vec_im)
    return jnp.stack([left_re, left_im], 1).astype(jnp.bfloat16)


def right_side(vectors, gamma_re, gamma_im):
    count = vectors.shape[1]
    width = vectors.shape[3]
    sol_re = vectors[0].astype(jnp.float32).reshape(count, 4, 3, width)
    sol_im = vectors[1].astype(jnp.float32).reshape(count, 4, 3, width)
    high = lax.Precision.HIGHEST
    rot_re = jnp.einsum("gst,xtcj->gxscj", gamma_re, sol_re, precision=high) - jnp.einsum(
        "gst,xtcj->gxscj", gamma_im, sol_im, precision=high
    )
    rot_im = jnp.einsum("gst,xtcj->gxscj", gamma_re, sol_im, precision=high) + jnp.einsum(
        "gst,xtcj->gxscj", gamma_im, sol_re, precision=high
    )
    groups = gamma_re.shape[0]
    rot_re = rot_re.reshape(groups, count, 12, width)
    rot_im = rot_im.reshape(groups, count, 12, width)
    upper = jnp.stack([rot_re, rot_im], 3)
    lower = jnp.stack([-rot_im, rot_re], 3)
    return jnp.stack([upper, lower], 1).astype(jnp.bfloat16)


def general_body(eigvecs, solutions, momenta, gammas):
    local_sites = eigvecs.shape[1]
    vec_count = eigvecs.shape[3]
    col_count = solutions.shape[3]
    groups = gammas.shape[0]
    mom_count = momenta.shape[0]
    device = lax.axis_index("space")
    space_count = lax.axis_size("space")
    gamma_re, gamma_im = select_gammas(gammas)
    cosine, sine_part = phases(momenta, device * local_sites, local_sites)
    left = left_side(eigvecs, cosine, sine_part)
    right = right_side(solutions, gamma_re, gamma_im)
    partial_fields = jnp.einsum(
        "paxci,gaxcrj->gpirj", left, right, preferred_element_type=jnp.float32
    )
    partial_fields = partial_fields.reshape(groups * mom_count * vec_count, 2, col_count)
    fields = lax.psum_scatter(partial_fields, "space", scatter_dimension=0, tiled=True)
    own_rows = fields.shape[0]
    spacing = space_count // groups
    own_gamma = device // spacing
    row_index = device * own_rows + jnp.arange(own_rows, dtype=jnp.int32)
    row_mom = row_index % (mom_count * vec_count) // vec_count
    mom_onehot = (row_mom[:, None] == jnp.arange(mom_count, dtype=jnp.int32)[None, :]).astype(
        jnp.float32
    )
    gamma_range = jnp.arange(groups, dtype=jnp.int32)

    def pair_terms(first_rows, second_rows):
        real_sum = jnp.sum(
            first_rows[:, 0] * second_rows[:, 0] + first_rows[:, 1] * second_rows[:, 1], -1
        )
        imag_sum = jnp.sum(
            first_rows[:, 1] * second_rows[:, 0] - first_rows[:, 0] * second_rows[:, 1], -1
        )
        return jnp.dot(
            mom_onehot.T, jnp.stack([real_sum, imag_sum], 1), precision=lax.Precision.HIGHEST
        )

    def place(row_gamma, col_gamma, values):
        row_hot = (gamma_range == row_gamma).astype(jnp.float32)
        col_hot = (gamma_range == col_gamma).astype(jnp.float32)
        return row_hot[:, None, None, None] * col_hot[None, :, None, None] * values[None, None]

    total = place(own_gamma, own_gamma, pair_terms(fields, fields))
    last_shift = groups - 1
    for step in range(1, last_shift + 1):
        other = shifted(fields.astype(jnp.bfloat16), "space", step * spacing).astype(fields.dtype)
        values = pair_terms(fields, other)
        other_gamma = (own_gamma - step) % groups
        total = total + place(own_gamma, other_gamma, values)
    traces = lax.psum(total, ("space", "mode")) / float(vec_count * vec_count)
    return (fields, traces)


def solution(mesh):
    fits = dict(mesh.shape) == {"space": 16, "mode": 2}
    if fits:
        cut = Mesh(mesh.devices.reshape(4, 2, 2, 2), ("z", "x", "core", "mode"))
        space = ("z", "x", "core")
    else:
        cut, space = mesh, "space"

    def step(eigvecs, solutions, momenta, gammas):
        sized = eigvecs.shape == (2, 512, 12, 384) and solutions.shape == (2, 512, 12, 384)
        sized = sized and momenta.shape == (8, 3) and gammas.shape == (4,)
        return jax.shard_map(
            fast_body if fits and sized else general_body,
            mesh=cut if fits and sized else mesh,
            in_specs=(
                P(None, space if fits and sized else "space", None, None),
                P(None, space if fits and sized else "space", None, "mode"),
                P(),
                P(),
            ),
            out_specs=(P(space if fits and sized else "space", None, "mode"), P()),
            check_vma=False,
        )(eigvecs, solutions, momenta, gammas)

    return step
```

```python
import functools
import math

import jax
import jax.numpy as jnp
import numpy as np
from jax import lax
from jax.experimental import pallas as pl
from jax.experimental.pallas import tpu as pltpu
from jax.sharding import Mesh
from jax.sharding import PartitionSpec as P

LATT = 96
VMEM = pl.BlockSpec(memory_space=pltpu.VMEM)
SMEM = pl.BlockSpec(memory_space=pltpu.SMEM)
HBM = pl.BlockSpec(memory_space=pltpu.HBM)
BF16 = jnp.bfloat16
F32 = jnp.float32


ORDER = (6, 4, 7, 5, 3, 2, 1)
COST = pl.CostEstimate(flops=2_000_000_000, bytes_accessed=8_000_000, transcendentals=0)


def gamma_table():
    unit = 1j
    first = np.array([[0, 0, 0, unit], [0, 0, unit, 0], [0, -unit, 0, 0], [-unit, 0, 0, 0]])
    second = np.array([[0, 0, 0, -1], [0, 0, 1, 0], [0, 1, 0, 0], [-1, 0, 0, 0]], dtype=complex)
    third = np.array([[0, 0, unit, 0], [0, 0, 0, -unit], [-unit, 0, 0, 0], [0, unit, 0, 0]])
    fourth = np.array([[0, 0, 1, 0], [0, 0, 0, 1], [1, 0, 0, 0], [0, 1, 0, 0]], dtype=complex)
    basis = [first, second, third, fourth]
    table = []
    for number in range(16):
        matrix = np.eye(4, dtype=complex)
        for bit_pos in range(4):
            if number >> bit_pos & 1:
                matrix = matrix @ basis[bit_pos]
        table.append(matrix)
    return np.stack(table)


def shift_lanes(x, by):
    by = by % x.shape[-1]
    return x if by == 0 else pltpu.roll(x, by, x.ndim - 1)


def by_quarter(lane, first, second, third, fourth):
    tiles = []
    for k, (low, high) in enumerate(((first, second), (second, third), (third, fourth))):
        at = slice(k * 128, (k + 1) * 128)
        tiles.append(jnp.where(lane[:, at] < (k + 1) * 96, wide(low, at), wide(high, at)))
    return jnp.concatenate(tiles, axis=1)


def wide(x, at):
    return x[:, at] if x.shape[1] > 1 else x


def here():
    return lax.axis_index("z"), lax.axis_index("x"), lax.axis_index("core")


def prepare_sol_kernel(sol, sol_own, sol_other, turned):
    x = lax.axis_index("x")
    for r in range(2):
        flipped = sol[r].astype(F32).T.astype(BF16)
        for k in range(2):
            turned[k, :, r * 384 : (r + 1) * 384] = flipped[k * 96 : (k + 1) * 96]
    sol_own[...] = turned[x]
    sol_other[...] = turned[x ^ 1]


def prepare_sol(sol):
    return pl.pallas_call(
        prepare_sol_kernel,
        out_shape=[jax.ShapeDtypeStruct((96, 768), BF16)] * 2,
        in_specs=[VMEM],
        out_specs=[VMEM] * 2,
        scratch_shapes=[pltpu.VMEM((2, 96, 768), BF16)],
        compiler_params=pltpu.CompilerParams(vmem_limit_bytes=16 << 20),
        cost_estimate=COST,
    )(sol)


def prepare_eig_kernel(eig, after, full, *rest):
    eig_out, packs = rest[:3], rest[3]
    z, half = lax.axis_index("z"), lax.axis_index("mode")
    lane = lax.broadcasted_iota(jnp.int32, (96, 384), 1)
    for side in range(2):
        at = side * 192
        parts = [
            eig[r, at + low * 96 : at + low * 96 + 96, :].astype(F32)
            for low in range(2)
            for r in range(2)
        ]
        for quarter in range(4):
            moved = [shift_lanes(part, 96 * (k - quarter)) for k, part in enumerate(parts)]
            packs[quarter, side] = by_quarter(lane, *moved).astype(BF16)
    full[0:96] = packs[z, 0]
    full[96:192] = packs[z, 1]
    for k in range(1, 4):
        eig_out[k - 1][...] = packs[z ^ k, half]


def site_phases(momenta, cosine, sine):
    z, x, core = here()
    shape = cosine.shape[::-1]
    mom = lax.broadcasted_iota(jnp.int32, shape, 0)
    lane = lax.broadcasted_iota(jnp.int32, shape, 1)
    device = (z * 4 + x * 2 + core) ^ ((lane >> 5) << 1)
    site = (device * 32 + (lane & 31)).astype(F32)
    line = jnp.floor((site + 0.5) * (1.0 / LATT))
    coord_x = jnp.floor((line + 0.5) * (1.0 / LATT))
    coords = (coord_x, line - LATT * coord_x, site - LATT * line)
    steps = jnp.zeros(shape, F32)
    for axis, coord in enumerate(coords):
        factor = jnp.zeros(shape, F32)
        for p in range(8):
            factor = jnp.where(mom == p, momenta[axis, p].astype(F32), factor)
        steps += factor * coord
    steps -= LATT * jnp.floor((steps + 0.5) * (1.0 / LATT))
    theta = 2.0 * math.pi / LATT * steps
    cosine[...] = jnp.cos(theta).T
    sine[...] = jnp.sin(theta).T


def prepare_eig(eig, after):
    return pl.pallas_call(
        prepare_eig_kernel,
        out_shape=[jax.ShapeDtypeStruct((192, 384), BF16)]
        + [jax.ShapeDtypeStruct((96, 384), BF16)] * 3,
        in_specs=[VMEM, HBM],
        out_specs=[VMEM] * 4,
        scratch_shapes=[pltpu.VMEM((4, 2, 96, 384), BF16)],
        compiler_params=pltpu.CompilerParams(vmem_limit_bytes=16 << 20),
    )(eig, after)


def build_base(first, second, base):
    lane = lax.broadcasted_iota(jnp.int32, (96, 384), 1)
    parts = [
        [plane[m, :, r * 384 : (r + 1) * 384] for plane in (first, second) for m in range(2)]
        for r in range(2)
    ]
    for t in range(4):
        re, im = [
            by_quarter(lane, *[shift_lanes(x, 96 * (k - t)) for k, x in enumerate(part)])
            for part in parts
        ]
        for turn, x in enumerate((re, -im, -re, im)):
            base[turn * 4 + t] = x


def build_left(base, gammas, table, left):
    for g in range(4):
        for part in range(2):
            at = g * 192 + part * 96
            for s in range(4):
                source = table[gammas[g] * 8 + part * 4 + s]
                left[at : at + 96, s * 384 : (s + 1) * 384] = base[source]


def build_phases(cosine, sine, at, phases):
    lane = lax.broadcasted_iota(jnp.int32, (32, 384), 1)
    for part, table in enumerate((cosine, sine)):
        rows = table[at : at + 32, :]
        for h in range(2):
            four = [rows[:, p : p + 1] for p in (2 * h, 2 * h + 1, 2 * h + 4, 2 * h + 5)]
            phases[h, part] = by_quarter(lane, *four)


def build_right(blocks, k, m, cosine, sine, right, phases, spread):
    lane = lax.broadcasted_iota(jnp.int32, (96, 384), 1)
    build_phases(cosine, sine, (k * 2 + m) * 32, phases)
    for side, (spin, block) in enumerate(blocks):
        w = block.astype(F32)
        turns = [shift_lanes(w, 96 * by) for by in range(4)]
        for part in range(4):
            x = by_quarter(lane, *[turns[(k4 - part) % 4] for k4 in range(4)])
            spread[side, part] = -x if part % 2 else x
    for h in range(2):
        cos, sin = phases[h, 0][None], phases[h, 1][None]
        for side, (spin, _) in enumerate(blocks):
            for low in range(2):
                re = spread[side, low * 2].reshape(3, 32, 384)
                im = spread[side, low * 2 + 1].reshape(3, 32, 384)
                at = (spin + low) * 384 + (k % 2) * 192 + m * 96
                rows = slice(at, at + 96)
                right[h, rows, 0:384] = (cos * re + sin * im).reshape(96, 384).astype(BF16)
                right[h, rows, 384:768] = (cos * im - sin * re).reshape(96, 384).astype(BF16)


def far_blocks(eigs, k, m):
    x = lax.axis_index("x")
    return [(half * 2, eigs[x ^ m, half, k - 1]) for half in range(2)]


def product(left, right, side, n):
    at = slice(n * 256, (n + 1) * 256)
    return at, jnp.dot(left[...], right[side, :, at], preferred_element_type=F32)


def near_kernel(gammas, table, momenta, *refs):
    sols, fulls, eigs, accs, far_right = refs[:2], refs[2:4], refs[4], refs[5:7], refs[7]
    base, left, right, phases, spread, cosine, sine = refs[8:]
    site_phases(momenta, cosine, sine)
    work = (phases, spread)
    for m in range(2):
        blocks = [(0, fulls[m][0:96]), (2, fulls[m][96:192])]
        build_right(blocks, 0, m, cosine, sine, right, *work)
    build_base(*sols, base)
    build_left(base, gammas, table, left)
    for k in range(1, 4):
        for m in range(2):
            build_right(far_blocks(eigs, k, m), k, m, cosine, sine, far_right if k > 1 else right, *work)
    core = lax.axis_index("core")
    for acc, side in ((accs[0], core), (accs[1], core ^ 1)):
        for n in range(3):
            at, part = product(left, right, side, n)
            acc[:, at] = part


def given_kernel(gammas, table, second, first, right, acc, out, left, base):
    build_base(first, second, base)
    build_left(base, gammas, table, left)
    for n in range(3):
        at, part = product(left, right, lax.axis_index("core") ^ 1, n)
        out[:, at] = (acc[:, at] + part).astype(BF16)


def own_kernel(left, right, acc, out):
    for n in range(3):
        at, part = product(left, right, lax.axis_index("core"), n)
        out[:, at] = acc[:, at] + part


def finish_kernel(own, got, *rest):
    outs, pairs = rest[:8], rest[8]
    z, x, _ = here()
    low = lax.broadcasted_iota(jnp.int32, (96, 384), 1) < 192
    gs, res, ims = [z ^ k for k in range(4)], [], []
    for k in range(4):
        (a, b), (c, d) = [
            [
                own[pl.ds(at, 96), lanes] + got[pl.ds(at, 96), lanes].astype(F32)
                for lanes in (slice(0, 384), slice(384, 768))
            ]
            for at in (pl.multiple_of(gs[k] * 192, 96), pl.multiple_of(gs[k] * 192 + 96, 96))
        ]
        re, im = a - d, b + c
        res.append(re)
        ims.append(im)
        first = jnp.where(low, re, shift_lanes(im, 192))
        second = jnp.where(low, shift_lanes(re, 192), im)
        for tile in range(3):
            lanes, rows = slice(tile * 128, (tile + 1) * 128), slice(tile * 96, (tile + 1) * 96)
            one, two = first[:, lanes], second[:, lanes]
            outs[k * 2][rows] = jnp.where(x == 0, one, two).astype(BF16)
            outs[k * 2 + 1][rows] = jnp.where(x == 0, two, one).astype(BF16)
    for i in range(4):
        for k in range(i, 4):
            at, mirror = (gs[i] * 4 + gs[k]) * 2, (gs[k] * 4 + gs[i]) * 2
            both = jnp.sum(res[i] * res[k] + ims[i] * ims[k], axis=0, keepdims=True)
            pairs[pl.ds(at, 1), :] = both
            if k > i:
                turn = jnp.sum(ims[i] * res[k] - res[i] * ims[k], axis=0, keepdims=True)
                pairs[pl.ds(mirror, 1), :] = both
                pairs[pl.ds(at + 1, 1), :] = turn
                pairs[pl.ds(mirror + 1, 1), :] = -turn
            else:
                pairs[pl.ds(at + 1, 1), :] = jnp.zeros_like(both)
    lane_p = lax.broadcasted_iota(jnp.int32, (8, 384), 1)
    mom = lax.broadcasted_iota(jnp.int32, (8, 384), 0)
    total = lax.dot_general(
        (lane_p // 96 == mom).astype(F32),
        pairs[...],
        (((1,), (1,)), ((), ())),
        precision=lax.Precision.HIGHEST,
        preferred_element_type=F32,
    )
    high = total.astype(BF16)
    low_part = (total - high.astype(F32)).astype(BF16)
    tail = jnp.concatenate([high, low_part, jnp.zeros((8, 64), BF16)], axis=1)
    for k in range(8):
        outs[k][288:296] = tail


BASE = pltpu.VMEM((16, 96, 384), BF16)
SPREAD = [pltpu.VMEM((2, 2, 32, 384), F32), pltpu.VMEM((2, 4, 96, 384), F32)]


def call(kernel, inputs, scalars, out_shape, scratch=(), limit=24):
    return pl.pallas_call(
        kernel,
        out_shape=out_shape,
        in_specs=[SMEM] * len(scalars) + [VMEM] * len(inputs),
        out_specs=jax.tree.map(lambda _: VMEM, out_shape),
        scratch_shapes=scratch,
        compiler_params=pltpu.CompilerParams(vmem_limit_bytes=limit << 20),
    )(*scalars, *inputs)


def join_kernel(*refs):
    got, out, blocks = refs[:8], refs[8], refs[9]
    z, x, _ = here()
    for k, block in zip((0,) + ORDER, got):
        for tile in range(3):
            lanes = slice(tile * 128, (tile + 1) * 128)
            blocks[(z ^ (k // 2)) * 2 + (x ^ (k % 2)), :, lanes] = block[tile * 96 : tile * 96 + 96]
    for side in range(2):
        rows = slice(side * 96, (side + 1) * 96)
        parts = [blocks[k * 2 + side].astype(F32) for k in range(4)]
        for r in range(2):
            for p in range(2):
                at = r * 192 + p * 96
                out[r, rows, p * 384 : (p + 1) * 384] = jnp.concatenate(
                    [part[:, at : at + 96] for part in parts], axis=1
                )


def traces_kernel(vec_count, own, core, own_mode, core_mode, out):
    mine, other = own[...] + own_mode[...], core[...] + core_mode[...]
    first = lax.axis_index("core") == 0
    low, high = jnp.where(first, mine, other), jnp.where(first, other, mine)
    rows = jnp.concatenate([low[0:2], high[0:2], low[2:4], high[2:4]], axis=0)
    rows = rows * (1.0 / float(vec_count * vec_count))
    turned = jnp.concatenate([rows, jnp.zeros((8, 96), F32)], axis=1).T
    for g in range(4):
        for k in range(4):
            at = (g * 4 + k) * 2
            out[g, k] = turned[at : at + 2]


def swap(x, axis, mask):
    return lax.ppermute(x, axis, [(i, i ^ mask) for i in range(lax.axis_size(axis))])


def fast_body(eigvecs, solutions, momenta, gammas):
    vec_count = eigvecs.shape[3]
    eig = eigvecs.transpose(0, 2, 1, 3).reshape(2, 384, 384)
    sol = solutions.transpose(0, 2, 1, 3).reshape(2, 384, 192)
    sol_own, sol_other = prepare_sol(sol)
    full, *eig_own = prepare_eig(eig, sol_other)
    sol_pair = jnp.stack([sol_own, swap(sol_other, "x", 1)])
    mine = jnp.stack([swap(eig_own[k - 1], "z", k) for k in range(1, 4)])
    sols = [sol_pair] + [swap(sol_pair, "z", k) for k in range(1, 4)]

    table = gamma_table()
    spin = np.argmax(np.abs(table), axis=2)
    turn = np.round(np.angle(table.sum(axis=2)) / (np.pi / 2)).astype(int) % 4
    rows = np.stack([turn * 4 + spin, (turn + 3) % 4 * 4 + spin], axis=1)
    scalars = (gammas, jnp.asarray(rows.astype(np.int32).reshape(128)))

    total = jax.ShapeDtypeStruct((768, 768), F32)
    left, right = pltpu.VMEM((768, 1536), BF16), (2, 1536, 768)
    eig_all = lax.all_gather(mine, ("x", "mode")).reshape(2, 2, 3, 96, 384)
    acc_own, acc_other, right = call(
        near_kernel,
        [*sols[:2], full, swap(full, "x", 1), eig_all],
        [*scalars, momenta.T],
        [total] * 2 + [jax.ShapeDtypeStruct(right, BF16)],
        [
            BASE,
            left,
            pltpu.VMEM(right, BF16),
            *SPREAD,
            pltpu.VMEM((256, 8), F32),
            pltpu.VMEM((256, 8), F32),
        ],
        36,
    )
    given, left = call(
        given_kernel,
        [sols[3], sols[2], right, acc_other],
        scalars,
        [jax.ShapeDtypeStruct((768, 768), BF16), jax.ShapeDtypeStruct((768, 1536), BF16)],
        [BASE],
    )
    taken = swap(given, "core", 1)
    own = call(own_kernel, [left, right, acc_own], [], total)
    sent = call(
        finish_kernel,
        [own, taken],
        [],
        [jax.ShapeDtypeStruct((296, 128), BF16)] * 8,
        [pltpu.VMEM((32, 384), F32)],
    )
    got = [sent[0]] + [swap(sent[k], ("z", "x"), k) for k in ORDER]
    part = sum(block[288:292, :64].astype(F32) for block in got)
    part = part[:, :32] + part[:, 32:]
    others = [swap(part, "core", 1), swap(part, "mode", 1), swap(part, ("core", "mode"), 3)]
    traces = call(
        functools.partial(traces_kernel, vec_count),
        [part, *others],
        [],
        jax.ShapeDtypeStruct((4, 4, 2, 8), F32),
    ).transpose(0, 1, 3, 2)
    fields = call(
        join_kernel,
        got,
        [],
        jax.ShapeDtypeStruct((2, 192, 768), F32),
        [pltpu.VMEM((8, 96, 384), BF16)],
    ).transpose(2, 0, 1)
    return fields, traces


def shifted(x, axis, by):
    count = lax.axis_size(axis)
    return lax.ppermute(x, axis, [(i, (i + by) % count) for i in range(count)])


def select_gammas(gammas):
    table = gamma_table()
    table_re, table_im = table.real.astype(np.float32), table.imag.astype(np.float32)
    select = (gammas[:, None] == jnp.arange(16, dtype=jnp.int32)[None, :]).astype(jnp.float32)
    count = gammas.shape[0]
    real_part = jnp.dot(
        select, jnp.asarray(table_re).reshape(16, 16), precision=lax.Precision.HIGHEST
    ).reshape(count, 4, 4)
    imag_part = jnp.dot(
        select, jnp.asarray(table_im).reshape(16, 16), precision=lax.Precision.HIGHEST
    ).reshape(count, 4, 4)
    return (real_part, imag_part)


def phases(momenta, first_site, count):
    index = first_site + jnp.arange(count, dtype=jnp.int32)
    coord_x = index // (LATT * LATT)
    coord_y = index // LATT % LATT
    coord_z = index % LATT
    phase_int = (
        momenta[:, 0:1] * coord_x[None, :]
        + momenta[:, 1:2] * coord_y[None, :]
        + momenta[:, 2:3] * coord_z[None, :]
    ) % LATT
    theta = 2.0 * math.pi / LATT * phase_int.astype(jnp.float32)
    return (jnp.cos(theta), jnp.sin(theta))


def left_side(vectors, cosine, sine_part):
    vec_re = vectors[0].astype(jnp.float32)[None]
    vec_im = vectors[1].astype(jnp.float32)[None]
    cosine = cosine[:, :, None, None]
    sine_part = sine_part[:, :, None, None]
    left_re = cosine * vec_re - sine_part * vec_im
    left_im = -(sine_part * vec_re + cosine * vec_im)
    return jnp.stack([left_re, left_im], 1).astype(jnp.bfloat16)


def right_side(vectors, gamma_re, gamma_im):
    count = vectors.shape[1]
    width = vectors.shape[3]
    sol_re = vectors[0].astype(jnp.float32).reshape(count, 4, 3, width)
    sol_im = vectors[1].astype(jnp.float32).reshape(count, 4, 3, width)
    high = lax.Precision.HIGHEST
    rot_re = jnp.einsum("gst,xtcj->gxscj", gamma_re, sol_re, precision=high) - jnp.einsum(
        "gst,xtcj->gxscj", gamma_im, sol_im, precision=high
    )
    rot_im = jnp.einsum("gst,xtcj->gxscj", gamma_re, sol_im, precision=high) + jnp.einsum(
        "gst,xtcj->gxscj", gamma_im, sol_re, precision=high
    )
    groups = gamma_re.shape[0]
    rot_re = rot_re.reshape(groups, count, 12, width)
    rot_im = rot_im.reshape(groups, count, 12, width)
    upper = jnp.stack([rot_re, rot_im], 3)
    lower = jnp.stack([-rot_im, rot_re], 3)
    return jnp.stack([upper, lower], 1).astype(jnp.bfloat16)


def general_body(eigvecs, solutions, momenta, gammas):
    local_sites = eigvecs.shape[1]
    vec_count = eigvecs.shape[3]
    col_count = solutions.shape[3]
    groups = gammas.shape[0]
    mom_count = momenta.shape[0]
    device = lax.axis_index("space")
    space_count = lax.axis_size("space")
    gamma_re, gamma_im = select_gammas(gammas)
    cosine, sine_part = phases(momenta, device * local_sites, local_sites)
    left = left_side(eigvecs, cosine, sine_part)
    right = right_side(solutions, gamma_re, gamma_im)
    partial_fields = jnp.einsum(
        "paxci,gaxcrj->gpirj", left, right, preferred_element_type=jnp.float32
    )
    partial_fields = partial_fields.reshape(groups * mom_count * vec_count, 2, col_count)
    fields = lax.psum_scatter(partial_fields, "space", scatter_dimension=0, tiled=True)
    own_rows = fields.shape[0]
    spacing = space_count // groups
    own_gamma = device // spacing
    row_index = device * own_rows + jnp.arange(own_rows, dtype=jnp.int32)
    row_mom = row_index % (mom_count * vec_count) // vec_count
    mom_onehot = (row_mom[:, None] == jnp.arange(mom_count, dtype=jnp.int32)[None, :]).astype(
        jnp.float32
    )
    gamma_range = jnp.arange(groups, dtype=jnp.int32)

    def pair_terms(first_rows, second_rows):
        real_sum = jnp.sum(
            first_rows[:, 0] * second_rows[:, 0] + first_rows[:, 1] * second_rows[:, 1], -1
        )
        imag_sum = jnp.sum(
            first_rows[:, 1] * second_rows[:, 0] - first_rows[:, 0] * second_rows[:, 1], -1
        )
        return jnp.dot(
            mom_onehot.T, jnp.stack([real_sum, imag_sum], 1), precision=lax.Precision.HIGHEST
        )

    def place(row_gamma, col_gamma, values):
        row_hot = (gamma_range == row_gamma).astype(jnp.float32)
        col_hot = (gamma_range == col_gamma).astype(jnp.float32)
        return row_hot[:, None, None, None] * col_hot[None, :, None, None] * values[None, None]

    total = place(own_gamma, own_gamma, pair_terms(fields, fields))
    last_shift = groups - 1
    for step in range(1, last_shift + 1):
        other = shifted(fields.astype(jnp.bfloat16), "space", step * spacing).astype(fields.dtype)
        values = pair_terms(fields, other)
        other_gamma = (own_gamma - step) % groups
        total = total + place(own_gamma, other_gamma, values)
    traces = lax.psum(total, ("space", "mode")) / float(vec_count * vec_count)
    return (fields, traces)


def solution(mesh):
    fits = dict(mesh.shape) == {"space": 16, "mode": 2}
    if fits:
        cut = Mesh(mesh.devices.reshape(4, 2, 2, 2), ("z", "x", "core", "mode"))
        space = ("z", "x", "core")
    else:
        cut, space = mesh, "space"

    def step(eigvecs, solutions, momenta, gammas):
        sized = eigvecs.shape == (2, 512, 12, 384) and solutions.shape == (2, 512, 12, 384)
        sized = sized and momenta.shape == (8, 3) and gammas.shape == (4,)
        return jax.shard_map(
            fast_body if fits and sized else general_body,
            mesh=cut if fits and sized else mesh,
            in_specs=(
                P(None, space if fits and sized else "space", None, None),
                P(None, space if fits and sized else "space", None, "mode"),
                P(),
                P(),
            ),
            out_specs=(P(space if fits and sized else "space", None, "mode"), P()),
            check_vma=False,
        )(eigvecs, solutions, momenta, gammas)

    return step
```

```python
import functools
import math

import jax
import jax.numpy as jnp
import numpy as np
from jax import lax
from jax.experimental import pallas as pl
from jax.experimental.pallas import tpu as pltpu
from jax.sharding import Mesh
from jax.sharding import PartitionSpec as P

LATT = 96
VMEM = pl.BlockSpec(memory_space=pltpu.VMEM)
SMEM = pl.BlockSpec(memory_space=pltpu.SMEM)
HBM = pl.BlockSpec(memory_space=pltpu.HBM)
BF16 = jnp.bfloat16
F32 = jnp.float32


ORDER = (6, 4, 2, 7, 5, 3, 1)
COST = pl.CostEstimate(flops=2_000_000_000, bytes_accessed=8_000_000, transcendentals=0)


def gamma_table():
    unit = 1j
    first = np.array([[0, 0, 0, unit], [0, 0, unit, 0], [0, -unit, 0, 0], [-unit, 0, 0, 0]])
    second = np.array([[0, 0, 0, -1], [0, 0, 1, 0], [0, 1, 0, 0], [-1, 0, 0, 0]], dtype=complex)
    third = np.array([[0, 0, unit, 0], [0, 0, 0, -unit], [-unit, 0, 0, 0], [0, unit, 0, 0]])
    fourth = np.array([[0, 0, 1, 0], [0, 0, 0, 1], [1, 0, 0, 0], [0, 1, 0, 0]], dtype=complex)
    basis = [first, second, third, fourth]
    table = []
    for number in range(16):
        matrix = np.eye(4, dtype=complex)
        for bit_pos in range(4):
            if number >> bit_pos & 1:
                matrix = matrix @ basis[bit_pos]
        table.append(matrix)
    return np.stack(table)


def shift_lanes(x, by):
    by = by % x.shape[-1]
    return x if by == 0 else pltpu.roll(x, by, x.ndim - 1)


def by_quarter(lane, first, second, third, fourth):
    tiles = []
    for k, (low, high) in enumerate(((first, second), (second, third), (third, fourth))):
        at = slice(k * 128, (k + 1) * 128)
        tiles.append(jnp.where(lane[:, at] < (k + 1) * 96, wide(low, at), wide(high, at)))
    return jnp.concatenate(tiles, axis=1)


def wide(x, at):
    return x[:, at] if x.shape[1] > 1 else x


def here():
    return lax.axis_index("z"), lax.axis_index("x"), lax.axis_index("core")


def prepare_sol_kernel(sol, sol_own, sol_other, turned):
    x = lax.axis_index("x")
    for r in range(2):
        flipped = sol[r].astype(F32).T.astype(BF16)
        for k in range(2):
            turned[k, :, r * 384 : (r + 1) * 384] = flipped[k * 96 : (k + 1) * 96]
    sol_own[...] = turned[x]
    sol_other[...] = turned[x ^ 1]


def prepare_sol(sol):
    return pl.pallas_call(
        prepare_sol_kernel,
        out_shape=[jax.ShapeDtypeStruct((96, 768), BF16)] * 2,
        in_specs=[VMEM],
        out_specs=[VMEM] * 2,
        scratch_shapes=[pltpu.VMEM((2, 96, 768), BF16)],
        compiler_params=pltpu.CompilerParams(vmem_limit_bytes=16 << 20),
        cost_estimate=COST,
    )(sol)


def prepare_eig_kernel(eig, after, full, *rest):
    eig_out, packs = rest[:3], rest[3]
    z, half = lax.axis_index("z"), lax.axis_index("mode")
    lane = lax.broadcasted_iota(jnp.int32, (96, 384), 1)
    for side in range(2):
        at = side * 192
        parts = [
            eig[r, at + low * 96 : at + low * 96 + 96, :].astype(F32)
            for low in range(2)
            for r in range(2)
        ]
        for quarter in range(4):
            moved = [shift_lanes(part, 96 * (k - quarter)) for k, part in enumerate(parts)]
            packs[quarter, side] = by_quarter(lane, *moved).astype(BF16)
    full[0:96] = packs[z, 0]
    full[96:192] = packs[z, 1]
    for k in range(1, 4):
        eig_out[k - 1][...] = packs[z ^ k, half]


def site_phases(momenta, cosine, sine):
    z, x, core = here()
    shape = cosine.shape[::-1]
    mom = lax.broadcasted_iota(jnp.int32, shape, 0)
    lane = lax.broadcasted_iota(jnp.int32, shape, 1)
    device = (z * 4 + x * 2 + core) ^ ((lane >> 5) << 1)
    site = (device * 32 + (lane & 31)).astype(F32)
    line = jnp.floor((site + 0.5) * (1.0 / LATT))
    coord_x = jnp.floor((line + 0.5) * (1.0 / LATT))
    coords = (coord_x, line - LATT * coord_x, site - LATT * line)
    steps = jnp.zeros(shape, F32)
    for axis, coord in enumerate(coords):
        factor = jnp.zeros(shape, F32)
        for p in range(8):
            factor = jnp.where(mom == p, momenta[axis, p].astype(F32), factor)
        steps += factor * coord
    steps -= LATT * jnp.floor((steps + 0.5) * (1.0 / LATT))
    theta = 2.0 * math.pi / LATT * steps
    cosine[...] = jnp.cos(theta).T
    sine[...] = jnp.sin(theta).T


def prepare_eig(eig, after):
    return pl.pallas_call(
        prepare_eig_kernel,
        out_shape=[jax.ShapeDtypeStruct((192, 384), BF16)]
        + [jax.ShapeDtypeStruct((96, 384), BF16)] * 3,
        in_specs=[VMEM, HBM],
        out_specs=[VMEM] * 4,
        scratch_shapes=[pltpu.VMEM((4, 2, 96, 384), BF16)],
        compiler_params=pltpu.CompilerParams(vmem_limit_bytes=16 << 20),
    )(eig, after)


def build_base(first, second, base):
    lane = lax.broadcasted_iota(jnp.int32, (96, 384), 1)
    parts = [
        [plane[m, :, r * 384 : (r + 1) * 384] for plane in (first, second) for m in range(2)]
        for r in range(2)
    ]
    for t in range(4):
        re, im = [
            by_quarter(lane, *[shift_lanes(x, 96 * (k - t)) for k, x in enumerate(part)])
            for part in parts
        ]
        for turn, x in enumerate((re, -im, -re, im)):
            base[turn * 4 + t] = x


def build_left(base, gammas, table, left):
    for g in range(4):
        for part in range(2):
            at = g * 192 + part * 96
            for s in range(4):
                source = table[gammas[g] * 8 + part * 4 + s]
                left[at : at + 96, s * 384 : (s + 1) * 384] = base[source]


def build_phases(cosine, sine, at, phases):
    lane = lax.broadcasted_iota(jnp.int32, (32, 384), 1)
    for part, table in enumerate((cosine, sine)):
        rows = table[at : at + 32, :]
        for h in range(2):
            four = [rows[:, p : p + 1] for p in (2 * h, 2 * h + 1, 2 * h + 4, 2 * h + 5)]
            phases[h, part] = by_quarter(lane, *four)


def build_right(blocks, k, m, cosine, sine, right, phases, spread):
    lane = lax.broadcasted_iota(jnp.int32, (96, 384), 1)
    build_phases(cosine, sine, (k * 2 + m) * 32, phases)
    for side, (spin, block) in enumerate(blocks):
        w = block.astype(F32)
        turns = [shift_lanes(w, 96 * by) for by in range(4)]
        for part in range(4):
            x = by_quarter(lane, *[turns[(k4 - part) % 4] for k4 in range(4)])
            spread[side, part] = -x if part % 2 else x
    for h in range(2):
        cos, sin = phases[h, 0][None], phases[h, 1][None]
        for side, (spin, _) in enumerate(blocks):
            for low in range(2):
                re = spread[side, low * 2].reshape(3, 32, 384)
                im = spread[side, low * 2 + 1].reshape(3, 32, 384)
                at = (spin + low) * 384 + (k % 2) * 192 + m * 96
                rows = slice(at, at + 96)
                right[h, rows, 0:384] = (cos * re + sin * im).reshape(96, 384).astype(BF16)
                right[h, rows, 384:768] = (cos * im - sin * re).reshape(96, 384).astype(BF16)


def far_blocks(eigs, k, m):
    x = lax.axis_index("x")
    return [(half * 2, eigs[x ^ m, half, k - 1]) for half in range(2)]


def product(left, right, side, n):
    at = slice(n * 256, (n + 1) * 256)
    return at, jnp.dot(left[...], right[side, :, at], preferred_element_type=F32)


def near_kernel(gammas, table, momenta, *refs):
    sols, fulls, eigs, accs, far_right = refs[:2], refs[2:4], refs[4], refs[5:7], refs[7]
    base, left, right, phases, spread, cosine, sine = refs[8:]
    site_phases(momenta, cosine, sine)
    work = (phases, spread)
    for m in range(2):
        blocks = [(0, fulls[m][0:96]), (2, fulls[m][96:192])]
        build_right(blocks, 0, m, cosine, sine, right, *work)
    build_base(*sols, base)
    build_left(base, gammas, table, left)
    for k in range(1, 4):
        for m in range(2):
            build_right(far_blocks(eigs, k, m), k, m, cosine, sine, far_right if k > 1 else right, *work)
    core = lax.axis_index("core")
    for acc, side in ((accs[0], core), (accs[1], core ^ 1)):
        for n in range(3):
            at, part = product(left, right, side, n)
            acc[:, at] = part


def given_kernel(gammas, table, second, first, right, acc, out, left, base):
    build_base(first, second, base)
    build_left(base, gammas, table, left)
    for n in range(3):
        at, part = product(left, right, lax.axis_index("core") ^ 1, n)
        out[:, at] = (acc[:, at] + part).astype(BF16)


def own_kernel(left, right, acc, out):
    for n in range(3):
        at, part = product(left, right, lax.axis_index("core"), n)
        out[:, at] = acc[:, at] + part


def finish_kernel(own, got, *rest):
    outs, pairs = rest[:8], rest[8]
    z, x, _ = here()
    low = lax.broadcasted_iota(jnp.int32, (96, 384), 1) < 192
    gs, res, ims = [z ^ k for k in range(4)], [], []
    for k in range(4):
        (a, b), (c, d) = [
            [
                own[pl.ds(at, 96), lanes] + got[pl.ds(at, 96), lanes].astype(F32)
                for lanes in (slice(0, 384), slice(384, 768))
            ]
            for at in (pl.multiple_of(gs[k] * 192, 96), pl.multiple_of(gs[k] * 192 + 96, 96))
        ]
        re, im = a - d, b + c
        res.append(re)
        ims.append(im)
        first = jnp.where(low, re, shift_lanes(im, 192))
        second = jnp.where(low, shift_lanes(re, 192), im)
        for tile in range(3):
            lanes, rows = slice(tile * 128, (tile + 1) * 128), slice(tile * 96, (tile + 1) * 96)
            one, two = first[:, lanes], second[:, lanes]
            outs[k * 2][rows] = jnp.where(x == 0, one, two).astype(BF16)
            outs[k * 2 + 1][rows] = jnp.where(x == 0, two, one).astype(BF16)
    for i in range(4):
        for k in range(i, 4):
            at, mirror = (gs[i] * 4 + gs[k]) * 2, (gs[k] * 4 + gs[i]) * 2
            both = jnp.sum(res[i] * res[k] + ims[i] * ims[k], axis=0, keepdims=True)
            pairs[pl.ds(at, 1), :] = both
            if k > i:
                turn = jnp.sum(ims[i] * res[k] - res[i] * ims[k], axis=0, keepdims=True)
                pairs[pl.ds(mirror, 1), :] = both
                pairs[pl.ds(at + 1, 1), :] = turn
                pairs[pl.ds(mirror + 1, 1), :] = -turn
            else:
                pairs[pl.ds(at + 1, 1), :] = jnp.zeros_like(both)
    lane_p = lax.broadcasted_iota(jnp.int32, (8, 384), 1)
    mom = lax.broadcasted_iota(jnp.int32, (8, 384), 0)
    total = lax.dot_general(
        (lane_p // 96 == mom).astype(F32),
        pairs[...],
        (((1,), (1,)), ((), ())),
        precision=lax.Precision.HIGHEST,
        preferred_element_type=F32,
    )
    high = total.astype(BF16)
    low_part = (total - high.astype(F32)).astype(BF16)
    tail = jnp.concatenate([high, low_part, jnp.zeros((8, 64), BF16)], axis=1)
    for k in range(8):
        outs[k][288:296] = tail


BASE = pltpu.VMEM((16, 96, 384), BF16)
SPREAD = [pltpu.VMEM((2, 2, 32, 384), F32), pltpu.VMEM((2, 4, 96, 384), F32)]


def call(kernel, inputs, scalars, out_shape, scratch=(), limit=24):
    return pl.pallas_call(
        kernel,
        out_shape=out_shape,
        in_specs=[SMEM] * len(scalars) + [VMEM] * len(inputs),
        out_specs=jax.tree.map(lambda _: VMEM, out_shape),
        scratch_shapes=scratch,
        compiler_params=pltpu.CompilerParams(vmem_limit_bytes=limit << 20),
    )(*scalars, *inputs)


def join_kernel(*refs):
    got, out, blocks = refs[:8], refs[8], refs[9]
    z, x, _ = here()
    for k, block in zip((0,) + ORDER, got):
        for tile in range(3):
            lanes = slice(tile * 128, (tile + 1) * 128)
            blocks[(z ^ (k // 2)) * 2 + (x ^ (k % 2)), :, lanes] = block[tile * 96 : tile * 96 + 96]
    for side in range(2):
        rows = slice(side * 96, (side + 1) * 96)
        parts = [blocks[k * 2 + side].astype(F32) for k in range(4)]
        for r in range(2):
            for p in range(2):
                at = r * 192 + p * 96
                out[r, rows, p * 384 : (p + 1) * 384] = jnp.concatenate(
                    [part[:, at : at + 96] for part in parts], axis=1
                )


def traces_kernel(vec_count, own, core, own_mode, core_mode, out):
    mine, other = own[...] + own_mode[...], core[...] + core_mode[...]
    first = lax.axis_index("core") == 0
    low, high = jnp.where(first, mine, other), jnp.where(first, other, mine)
    rows = jnp.concatenate([low[0:2], high[0:2], low[2:4], high[2:4]], axis=0)
    rows = rows * (1.0 / float(vec_count * vec_count))
    turned = jnp.concatenate([rows, jnp.zeros((8, 96), F32)], axis=1).T
    for g in range(4):
        for k in range(4):
            at = (g * 4 + k) * 2
            out[g, k] = turned[at : at + 2]


def swap(x, axis, mask):
    return lax.ppermute(x, axis, [(i, i ^ mask) for i in range(lax.axis_size(axis))])


def fast_body(eigvecs, solutions, momenta, gammas):
    vec_count = eigvecs.shape[3]
    eig = eigvecs.transpose(0, 2, 1, 3).reshape(2, 384, 384)
    sol = solutions.transpose(0, 2, 1, 3).reshape(2, 384, 192)
    sol_own, sol_other = prepare_sol(sol)
    full, *eig_own = prepare_eig(eig, sol_other)
    sol_pair = jnp.stack([sol_own, swap(sol_other, "x", 1)])
    mine = jnp.stack([swap(eig_own[k - 1], "z", k) for k in range(1, 4)])
    sols = [sol_pair] + [swap(sol_pair, "z", k) for k in range(1, 4)]

    table = gamma_table()
    spin = np.argmax(np.abs(table), axis=2)
    turn = np.round(np.angle(table.sum(axis=2)) / (np.pi / 2)).astype(int) % 4
    rows = np.stack([turn * 4 + spin, (turn + 3) % 4 * 4 + spin], axis=1)
    scalars = (gammas, jnp.asarray(rows.astype(np.int32).reshape(128)))

    total = jax.ShapeDtypeStruct((768, 768), F32)
    left, right = pltpu.VMEM((768, 1536), BF16), (2, 1536, 768)
    eig_all = lax.all_gather(mine, ("x", "mode")).reshape(2, 2, 3, 96, 384)
    acc_own, acc_other, right = call(
        near_kernel,
        [*sols[:2], full, swap(full, "x", 1), eig_all],
        [*scalars, momenta.T],
        [total] * 2 + [jax.ShapeDtypeStruct(right, BF16)],
        [
            BASE,
            left,
            pltpu.VMEM(right, BF16),
            *SPREAD,
            pltpu.VMEM((256, 8), F32),
            pltpu.VMEM((256, 8), F32),
        ],
        36,
    )
    given, left = call(
        given_kernel,
        [sols[3], sols[2], right, acc_other],
        scalars,
        [jax.ShapeDtypeStruct((768, 768), BF16), jax.ShapeDtypeStruct((768, 1536), BF16)],
        [BASE],
    )
    taken = swap(given, "core", 1)
    own = call(own_kernel, [left, right, acc_own], [], total)
    sent = call(
        finish_kernel,
        [own, taken],
        [],
        [jax.ShapeDtypeStruct((296, 128), BF16)] * 8,
        [pltpu.VMEM((32, 384), F32)],
    )
    got = [sent[0]] + [swap(sent[k], ("z", "x"), k) for k in ORDER]
    part = sum(block[288:292, :64].astype(F32) for block in got)
    part = part[:, :32] + part[:, 32:]
    others = [swap(part, "core", 1), swap(part, "mode", 1), swap(part, ("core", "mode"), 3)]
    traces = call(
        functools.partial(traces_kernel, vec_count),
        [part, *others],
        [],
        jax.ShapeDtypeStruct((4, 4, 2, 8), F32),
    ).transpose(0, 1, 3, 2)
    fields = call(
        join_kernel,
        got,
        [],
        jax.ShapeDtypeStruct((2, 192, 768), F32),
        [pltpu.VMEM((8, 96, 384), BF16)],
    ).transpose(2, 0, 1)
    return fields, traces


def shifted(x, axis, by):
    count = lax.axis_size(axis)
    return lax.ppermute(x, axis, [(i, (i + by) % count) for i in range(count)])


def select_gammas(gammas):
    table = gamma_table()
    table_re, table_im = table.real.astype(np.float32), table.imag.astype(np.float32)
    select = (gammas[:, None] == jnp.arange(16, dtype=jnp.int32)[None, :]).astype(jnp.float32)
    count = gammas.shape[0]
    real_part = jnp.dot(
        select, jnp.asarray(table_re).reshape(16, 16), precision=lax.Precision.HIGHEST
    ).reshape(count, 4, 4)
    imag_part = jnp.dot(
        select, jnp.asarray(table_im).reshape(16, 16), precision=lax.Precision.HIGHEST
    ).reshape(count, 4, 4)
    return (real_part, imag_part)


def phases(momenta, first_site, count):
    index = first_site + jnp.arange(count, dtype=jnp.int32)
    coord_x = index // (LATT * LATT)
    coord_y = index // LATT % LATT
    coord_z = index % LATT
    phase_int = (
        momenta[:, 0:1] * coord_x[None, :]
        + momenta[:, 1:2] * coord_y[None, :]
        + momenta[:, 2:3] * coord_z[None, :]
    ) % LATT
    theta = 2.0 * math.pi / LATT * phase_int.astype(jnp.float32)
    return (jnp.cos(theta), jnp.sin(theta))


def left_side(vectors, cosine, sine_part):
    vec_re = vectors[0].astype(jnp.float32)[None]
    vec_im = vectors[1].astype(jnp.float32)[None]
    cosine = cosine[:, :, None, None]
    sine_part = sine_part[:, :, None, None]
    left_re = cosine * vec_re - sine_part * vec_im
    left_im = -(sine_part * vec_re + cosine * vec_im)
    return jnp.stack([left_re, left_im], 1).astype(jnp.bfloat16)


def right_side(vectors, gamma_re, gamma_im):
    count = vectors.shape[1]
    width = vectors.shape[3]
    sol_re = vectors[0].astype(jnp.float32).reshape(count, 4, 3, width)
    sol_im = vectors[1].astype(jnp.float32).reshape(count, 4, 3, width)
    high = lax.Precision.HIGHEST
    rot_re = jnp.einsum("gst,xtcj->gxscj", gamma_re, sol_re, precision=high) - jnp.einsum(
        "gst,xtcj->gxscj", gamma_im, sol_im, precision=high
    )
    rot_im = jnp.einsum("gst,xtcj->gxscj", gamma_re, sol_im, precision=high) + jnp.einsum(
        "gst,xtcj->gxscj", gamma_im, sol_re, precision=high
    )
    groups = gamma_re.shape[0]
    rot_re = rot_re.reshape(groups, count, 12, width)
    rot_im = rot_im.reshape(groups, count, 12, width)
    upper = jnp.stack([rot_re, rot_im], 3)
    lower = jnp.stack([-rot_im, rot_re], 3)
    return jnp.stack([upper, lower], 1).astype(jnp.bfloat16)


def general_body(eigvecs, solutions, momenta, gammas):
    local_sites = eigvecs.shape[1]
    vec_count = eigvecs.shape[3]
    col_count = solutions.shape[3]
    groups = gammas.shape[0]
    mom_count = momenta.shape[0]
    device = lax.axis_index("space")
    space_count = lax.axis_size("space")
    gamma_re, gamma_im = select_gammas(gammas)
    cosine, sine_part = phases(momenta, device * local_sites, local_sites)
    left = left_side(eigvecs, cosine, sine_part)
    right = right_side(solutions, gamma_re, gamma_im)
    partial_fields = jnp.einsum(
        "paxci,gaxcrj->gpirj", left, right, preferred_element_type=jnp.float32
    )
    partial_fields = partial_fields.reshape(groups * mom_count * vec_count, 2, col_count)
    fields = lax.psum_scatter(partial_fields, "space", scatter_dimension=0, tiled=True)
    own_rows = fields.shape[0]
    spacing = space_count // groups
    own_gamma = device // spacing
    row_index = device * own_rows + jnp.arange(own_rows, dtype=jnp.int32)
    row_mom = row_index % (mom_count * vec_count) // vec_count
    mom_onehot = (row_mom[:, None] == jnp.arange(mom_count, dtype=jnp.int32)[None, :]).astype(
        jnp.float32
    )
    gamma_range = jnp.arange(groups, dtype=jnp.int32)

    def pair_terms(first_rows, second_rows):
        real_sum = jnp.sum(
            first_rows[:, 0] * second_rows[:, 0] + first_rows[:, 1] * second_rows[:, 1], -1
        )
        imag_sum = jnp.sum(
            first_rows[:, 1] * second_rows[:, 0] - first_rows[:, 0] * second_rows[:, 1], -1
        )
        return jnp.dot(
            mom_onehot.T, jnp.stack([real_sum, imag_sum], 1), precision=lax.Precision.HIGHEST
        )

    def place(row_gamma, col_gamma, values):
        row_hot = (gamma_range == row_gamma).astype(jnp.float32)
        col_hot = (gamma_range == col_gamma).astype(jnp.float32)
        return row_hot[:, None, None, None] * col_hot[None, :, None, None] * values[None, None]

    total = place(own_gamma, own_gamma, pair_terms(fields, fields))
    last_shift = groups - 1
    for step in range(1, last_shift + 1):
        other = shifted(fields.astype(jnp.bfloat16), "space", step * spacing).astype(fields.dtype)
        values = pair_terms(fields, other)
        other_gamma = (own_gamma - step) % groups
        total = total + place(own_gamma, other_gamma, values)
    traces = lax.psum(total, ("space", "mode")) / float(vec_count * vec_count)
    return (fields, traces)


def solution(mesh):
    fits = dict(mesh.shape) == {"space": 16, "mode": 2}
    if fits:
        cut = Mesh(mesh.devices.reshape(4, 2, 2, 2), ("z", "x", "core", "mode"))
        space = ("z", "x", "core")
    else:
        cut, space = mesh, "space"

    def step(eigvecs, solutions, momenta, gammas):
        sized = eigvecs.shape == (2, 512, 12, 384) and solutions.shape == (2, 512, 12, 384)
        sized = sized and momenta.shape == (8, 3) and gammas.shape == (4,)
        return jax.shard_map(
            fast_body if fits and sized else general_body,
            mesh=cut if fits and sized else mesh,
            in_specs=(
                P(None, space if fits and sized else "space", None, None),
                P(None, space if fits and sized else "space", None, "mode"),
                P(),
                P(),
            ),
            out_specs=(P(space if fits and sized else "space", None, "mode"), P()),
            check_vma=False,
        )(eigvecs, solutions, momenta, gammas)

    return step
```

```python
import functools
import math

import jax
import jax.numpy as jnp
import numpy as np
from jax import lax
from jax.experimental import pallas as pl
from jax.experimental.pallas import tpu as pltpu
from jax.sharding import Mesh
from jax.sharding import PartitionSpec as P

LATT = 96
VMEM = pl.BlockSpec(memory_space=pltpu.VMEM)
SMEM = pl.BlockSpec(memory_space=pltpu.SMEM)
HBM = pl.BlockSpec(memory_space=pltpu.HBM)
BF16 = jnp.bfloat16
F32 = jnp.float32


ORDER = (6, 4, 2, 7, 5, 3, 1)
COST = pl.CostEstimate(flops=2_000_000_000, bytes_accessed=8_000_000, transcendentals=0)


def gamma_table():
    unit = 1j
    first = np.array([[0, 0, 0, unit], [0, 0, unit, 0], [0, -unit, 0, 0], [-unit, 0, 0, 0]])
    second = np.array([[0, 0, 0, -1], [0, 0, 1, 0], [0, 1, 0, 0], [-1, 0, 0, 0]], dtype=complex)
    third = np.array([[0, 0, unit, 0], [0, 0, 0, -unit], [-unit, 0, 0, 0], [0, unit, 0, 0]])
    fourth = np.array([[0, 0, 1, 0], [0, 0, 0, 1], [1, 0, 0, 0], [0, 1, 0, 0]], dtype=complex)
    basis = [first, second, third, fourth]
    table = []
    for number in range(16):
        matrix = np.eye(4, dtype=complex)
        for bit_pos in range(4):
            if number >> bit_pos & 1:
                matrix = matrix @ basis[bit_pos]
        table.append(matrix)
    return np.stack(table)


def shift_lanes(x, by):
    by = by % x.shape[-1]
    return x if by == 0 else pltpu.roll(x, by, x.ndim - 1)


def by_quarter(lane, first, second, third, fourth):
    tiles = []
    for k, (low, high) in enumerate(((first, second), (second, third), (third, fourth))):
        at = slice(k * 128, (k + 1) * 128)
        tiles.append(jnp.where(lane[:, at] < (k + 1) * 96, wide(low, at), wide(high, at)))
    return jnp.concatenate(tiles, axis=1)


def wide(x, at):
    return x[:, at] if x.shape[1] > 1 else x


def here():
    return lax.axis_index("z"), lax.axis_index("x"), lax.axis_index("core")


def prepare_sol_kernel(sol, sol_own, sol_other, turned):
    x = lax.axis_index("x")
    for r in range(2):
        flipped = sol[r].astype(F32).T.astype(BF16)
        for k in range(2):
            turned[k, :, r * 384 : (r + 1) * 384] = flipped[k * 96 : (k + 1) * 96]
    sol_own[...] = turned[x]
    sol_other[...] = turned[x ^ 1]


def prepare_sol(sol):
    return pl.pallas_call(
        prepare_sol_kernel,
        out_shape=[jax.ShapeDtypeStruct((96, 768), BF16)] * 2,
        in_specs=[VMEM],
        out_specs=[VMEM] * 2,
        scratch_shapes=[pltpu.VMEM((2, 96, 768), BF16)],
        compiler_params=pltpu.CompilerParams(vmem_limit_bytes=16 << 20),
        cost_estimate=COST,
    )(sol)


def prepare_eig_kernel(eig, after, full, *rest):
    eig_out, packs = rest[:3], rest[3]
    z, half = lax.axis_index("z"), lax.axis_index("mode")
    lane = lax.broadcasted_iota(jnp.int32, (96, 384), 1)
    for side in range(2):
        at = side * 192
        parts = [
            eig[r, at + low * 96 : at + low * 96 + 96, :].astype(F32)
            for low in range(2)
            for r in range(2)
        ]
        for quarter in range(4):
            moved = [shift_lanes(part, 96 * (k - quarter)) for k, part in enumerate(parts)]
            packs[quarter, side] = by_quarter(lane, *moved).astype(BF16)
    full[0:96] = packs[z, 0]
    full[96:192] = packs[z, 1]
    for k in range(1, 4):
        eig_out[k - 1][...] = packs[z ^ k, half]


def site_phases(momenta, cosine, sine):
    z, x, core = here()
    shape = cosine.shape[::-1]
    mom = lax.broadcasted_iota(jnp.int32, shape, 0)
    lane = lax.broadcasted_iota(jnp.int32, shape, 1)
    device = (z * 4 + x * 2 + core) ^ ((lane >> 5) << 1)
    site = (device * 32 + (lane & 31)).astype(F32)
    line = jnp.floor((site + 0.5) * (1.0 / LATT))
    coord_x = jnp.floor((line + 0.5) * (1.0 / LATT))
    coords = (coord_x, line - LATT * coord_x, site - LATT * line)
    steps = jnp.zeros(shape, F32)
    for axis, coord in enumerate(coords):
        factor = jnp.zeros(shape, F32)
        for p in range(8):
            factor = jnp.where(mom == p, momenta[axis, p].astype(F32), factor)
        steps += factor * coord
    steps -= LATT * jnp.floor((steps + 0.5) * (1.0 / LATT))
    theta = 2.0 * math.pi / LATT * steps
    cosine[...] = jnp.cos(theta).T
    sine[...] = jnp.sin(theta).T


def prepare_eig(eig, after):
    return pl.pallas_call(
        prepare_eig_kernel,
        out_shape=[jax.ShapeDtypeStruct((192, 384), BF16)]
        + [jax.ShapeDtypeStruct((96, 384), BF16)] * 3,
        in_specs=[VMEM, HBM],
        out_specs=[VMEM] * 4,
        scratch_shapes=[pltpu.VMEM((4, 2, 96, 384), BF16)],
        compiler_params=pltpu.CompilerParams(vmem_limit_bytes=16 << 20),
    )(eig, after)


def build_base(first, second, base):
    lane = lax.broadcasted_iota(jnp.int32, (96, 384), 1)
    parts = [
        [plane[m, :, r * 384 : (r + 1) * 384] for plane in (first, second) for m in range(2)]
        for r in range(2)
    ]
    for t in range(4):
        re, im = [
            by_quarter(lane, *[shift_lanes(x, 96 * (k - t)) for k, x in enumerate(part)])
            for part in parts
        ]
        for turn, x in enumerate((re, -im, -re, im)):
            base[turn * 4 + t] = x


def build_left(base, gammas, table, left):
    for g in range(4):
        for part in range(2):
            at = g * 192 + part * 96
            for s in range(4):
                source = table[gammas[g] * 8 + part * 4 + s]
                left[at : at + 96, s * 384 : (s + 1) * 384] = base[source]


def build_phases(cosine, sine, at, phases):
    lane = lax.broadcasted_iota(jnp.int32, (32, 384), 1)
    for part, table in enumerate((cosine, sine)):
        rows = table[at : at + 32, :]
        for h in range(2):
            four = [rows[:, p : p + 1] for p in (2 * h, 2 * h + 1, 2 * h + 4, 2 * h + 5)]
            phases[h, part] = by_quarter(lane, *four)


def build_right(blocks, k, m, cosine, sine, right, phases, spread):
    lane = lax.broadcasted_iota(jnp.int32, (96, 384), 1)
    build_phases(cosine, sine, (k * 2 + m) * 32, phases)
    for spin, block in blocks:
        w = block.astype(F32)
        turns = [shift_lanes(w, 96 * by) for by in range(4)]
        copies = [
            by_quarter(lane, *[turns[(k4 - part) % 4] for k4 in range(4)]).reshape(3, 32, 384)
            for part in range(4)
        ]
        for low in range(2):
            re, im = copies[low * 2], -copies[low * 2 + 1]
            for h in range(2):
                cos, sin = phases[h, 0][None], phases[h, 1][None]
                at = (spin + low) * 384 + (k % 2) * 192 + m * 96
                rows = slice(at, at + 96)
                right[h, rows, 0:384] = (cos * re + sin * im).reshape(96, 384).astype(BF16)
                right[h, rows, 384:768] = (cos * im - sin * re).reshape(96, 384).astype(BF16)


def far_blocks(eigs, k, m):
    x = lax.axis_index("x")
    return [(half * 2, eigs[x ^ m, half, k - 1]) for half in range(2)]


def product(left, right, side, n):
    at = slice(n * 256, (n + 1) * 256)
    return at, jnp.dot(left[...], right[side, :, at], preferred_element_type=F32)


def near_kernel(gammas, table, momenta, *refs):
    sols, fulls, eigs, accs, far_right = refs[:2], refs[2:4], refs[4], refs[5:7], refs[7]
    base, left, right, phases, spread, cosine, sine = refs[8:]
    site_phases(momenta, cosine, sine)
    work = (phases, spread)
    for m in range(2):
        blocks = [(0, fulls[m][0:96]), (2, fulls[m][96:192])]
        build_right(blocks, 0, m, cosine, sine, right, *work)
    build_base(*sols, base)
    build_left(base, gammas, table, left)
    for k in range(1, 4):
        for m in range(2):
            build_right(far_blocks(eigs, k, m), k, m, cosine, sine, far_right if k > 1 else right, *work)
    core = lax.axis_index("core")
    for acc, side in ((accs[0], core), (accs[1], core ^ 1)):
        for n in range(3):
            at, part = product(left, right, side, n)
            acc[:, at] = part


def given_kernel(gammas, table, second, first, right, acc, out, left, base):
    build_base(first, second, base)
    build_left(base, gammas, table, left)
    for n in range(2):
        at, part = product(left, right, lax.axis_index("core") ^ 1, n)
        out[:, at] = (acc[:, at] + part).astype(BF16)


def rest_kernel(left, right, acc, out):
    at, part = product(left, right, lax.axis_index("core") ^ 1, 2)
    out[...] = (acc[:, at] + part).astype(BF16)


def own_kernel(left, right, acc, out):
    for n in range(3):
        at, part = product(left, right, lax.axis_index("core"), n)
        out[:, at] = acc[:, at] + part


def finish_kernel(own, got, got_rest, *rest):
    outs, pairs = rest[:8], rest[8]
    z, x, _ = here()
    low = lax.broadcasted_iota(jnp.int32, (96, 384), 1) < 192
    gs, res, ims = [z ^ k for k in range(4)], [], []
    for k in range(4):
        (a, b), (c, d) = [
            [
                own[pl.ds(at, 96), :384] + got[pl.ds(at, 96), :384].astype(F32),
                own[pl.ds(at, 96), 384:]
                + jnp.concatenate(
                    [got[pl.ds(at, 96), 384:].astype(F32), got_rest[pl.ds(at, 96), :].astype(F32)],
                    axis=1,
                ),
            ]
            for at in (pl.multiple_of(gs[k] * 192, 96), pl.multiple_of(gs[k] * 192 + 96, 96))
        ]
        re, im = a - d, b + c
        res.append(re)
        ims.append(im)
        first = jnp.where(low, re, shift_lanes(im, 192))
        second = jnp.where(low, shift_lanes(re, 192), im)
        for tile in range(3):
            lanes, rows = slice(tile * 128, (tile + 1) * 128), slice(tile * 96, (tile + 1) * 96)
            one, two = first[:, lanes], second[:, lanes]
            outs[k * 2][rows] = jnp.where(x == 0, one, two).astype(BF16)
            outs[k * 2 + 1][rows] = jnp.where(x == 0, two, one).astype(BF16)
    for i in range(4):
        for k in range(i, 4):
            at, mirror = (gs[i] * 4 + gs[k]) * 2, (gs[k] * 4 + gs[i]) * 2
            both = jnp.sum(res[i] * res[k] + ims[i] * ims[k], axis=0, keepdims=True)
            pairs[pl.ds(at, 1), :] = both
            if k > i:
                turn = jnp.sum(ims[i] * res[k] - res[i] * ims[k], axis=0, keepdims=True)
                pairs[pl.ds(mirror, 1), :] = both
                pairs[pl.ds(at + 1, 1), :] = turn
                pairs[pl.ds(mirror + 1, 1), :] = -turn
            else:
                pairs[pl.ds(at + 1, 1), :] = jnp.zeros_like(both)
    lane_p = lax.broadcasted_iota(jnp.int32, (8, 384), 1)
    mom = lax.broadcasted_iota(jnp.int32, (8, 384), 0)
    total = lax.dot_general(
        (lane_p // 96 == mom).astype(F32),
        pairs[...],
        (((1,), (1,)), ((), ())),
        precision=lax.Precision.HIGHEST,
        preferred_element_type=F32,
    )
    high = total.astype(BF16)
    low_part = (total - high.astype(F32)).astype(BF16)
    tail = jnp.concatenate([high, low_part, jnp.zeros((8, 64), BF16)], axis=1)
    for k in range(8):
        outs[k][288:296] = tail


BASE = pltpu.VMEM((16, 96, 384), BF16)
SPREAD = [pltpu.VMEM((2, 2, 32, 384), F32), pltpu.VMEM((2, 4, 96, 384), F32)]


def call(kernel, inputs, scalars, out_shape, scratch=(), limit=24):
    return pl.pallas_call(
        kernel,
        out_shape=out_shape,
        in_specs=[SMEM] * len(scalars) + [VMEM] * len(inputs),
        out_specs=jax.tree.map(lambda _: VMEM, out_shape),
        scratch_shapes=scratch,
        compiler_params=pltpu.CompilerParams(vmem_limit_bytes=limit << 20),
    )(*scalars, *inputs)


def join_kernel(*refs):
    got, out, blocks = refs[:8], refs[8], refs[9]
    z, x, _ = here()
    for k, block in zip((0,) + ORDER, got):
        for tile in range(3):
            lanes = slice(tile * 128, (tile + 1) * 128)
            blocks[(z ^ (k // 2)) * 2 + (x ^ (k % 2)), :, lanes] = block[tile * 96 : tile * 96 + 96]
    for side in range(2):
        rows = slice(side * 96, (side + 1) * 96)
        parts = [blocks[k * 2 + side].astype(F32) for k in range(4)]
        for r in range(2):
            for p in range(2):
                at = r * 192 + p * 96
                out[r, rows, p * 384 : (p + 1) * 384] = jnp.concatenate(
                    [part[:, at : at + 96] for part in parts], axis=1
                )


def traces_kernel(vec_count, own, core, own_mode, core_mode, out):
    mine, other = own[...] + own_mode[...], core[...] + core_mode[...]
    first = lax.axis_index("core") == 0
    low, high = jnp.where(first, mine, other), jnp.where(first, other, mine)
    rows = jnp.concatenate([low[0:2], high[0:2], low[2:4], high[2:4]], axis=0)
    rows = rows * (1.0 / float(vec_count * vec_count))
    turned = jnp.concatenate([rows, jnp.zeros((8, 96), F32)], axis=1).T
    for g in range(4):
        for k in range(4):
            at = (g * 4 + k) * 2
            out[g, k] = turned[at : at + 2]


def swap(x, axis, mask):
    return lax.ppermute(x, axis, [(i, i ^ mask) for i in range(lax.axis_size(axis))])


def fast_body(eigvecs, solutions, momenta, gammas):
    vec_count = eigvecs.shape[3]
    eig = eigvecs.transpose(0, 2, 1, 3).reshape(2, 384, 384)
    sol = solutions.transpose(0, 2, 1, 3).reshape(2, 384, 192)
    sol_own, sol_other = prepare_sol(sol)
    full, *eig_own = prepare_eig(eig, sol_other)
    sol_pair = jnp.stack([sol_own, swap(sol_other, "x", 1)])
    mine = jnp.stack([swap(eig_own[k - 1], "z", k) for k in range(1, 4)])
    sols = [sol_pair] + [swap(sol_pair, "z", k) for k in range(1, 4)]

    table = gamma_table()
    spin = np.argmax(np.abs(table), axis=2)
    turn = np.round(np.angle(table.sum(axis=2)) / (np.pi / 2)).astype(int) % 4
    rows = np.stack([turn * 4 + spin, (turn + 3) % 4 * 4 + spin], axis=1)
    scalars = (gammas, jnp.asarray(rows.astype(np.int32).reshape(128)))

    total = jax.ShapeDtypeStruct((768, 768), F32)
    left, right = pltpu.VMEM((768, 1536), BF16), (2, 1536, 768)
    eig_all = lax.all_gather(mine, ("x", "mode")).reshape(2, 2, 3, 96, 384)
    acc_own, acc_other, right = call(
        near_kernel,
        [*sols[:2], full, swap(full, "x", 1), eig_all],
        [*scalars, momenta.T],
        [total] * 2 + [jax.ShapeDtypeStruct(right, BF16)],
        [
            BASE,
            left,
            pltpu.VMEM(right, BF16),
            *SPREAD,
            pltpu.VMEM((256, 8), F32),
            pltpu.VMEM((256, 8), F32),
        ],
        36,
    )
    given, left = call(
        given_kernel,
        [sols[3], sols[2], right, acc_other],
        scalars,
        [jax.ShapeDtypeStruct((768, 512), BF16), jax.ShapeDtypeStruct((768, 1536), BF16)],
        [BASE],
    )
    given_rest = call(
        rest_kernel, [left, right, acc_other], [], jax.ShapeDtypeStruct((768, 256), BF16)
    )
    taken = [swap(given, "core", 1), swap(given_rest, "core", 1)]
    own = call(own_kernel, [left, right, acc_own], [], total)
    sent = call(
        finish_kernel,
        [own, *taken],
        [],
        [jax.ShapeDtypeStruct((296, 128), BF16)] * 8,
        [pltpu.VMEM((32, 384), F32)],
    )
    got = [sent[0]] + [swap(sent[k], ("z", "x"), k) for k in ORDER]
    part = sum(block[288:292, :64].astype(F32) for block in got)
    part = part[:, :32] + part[:, 32:]
    others = [swap(part, "core", 1), swap(part, "mode", 1), swap(part, ("core", "mode"), 3)]
    traces = call(
        functools.partial(traces_kernel, vec_count),
        [part, *others],
        [],
        jax.ShapeDtypeStruct((4, 4, 2, 8), F32),
    ).transpose(0, 1, 3, 2)
    fields = call(
        join_kernel,
        got,
        [],
        jax.ShapeDtypeStruct((2, 192, 768), F32),
        [pltpu.VMEM((8, 96, 384), BF16)],
    ).transpose(2, 0, 1)
    return fields, traces


def shifted(x, axis, by):
    count = lax.axis_size(axis)
    return lax.ppermute(x, axis, [(i, (i + by) % count) for i in range(count)])


def select_gammas(gammas):
    table = gamma_table()
    table_re, table_im = table.real.astype(np.float32), table.imag.astype(np.float32)
    select = (gammas[:, None] == jnp.arange(16, dtype=jnp.int32)[None, :]).astype(jnp.float32)
    count = gammas.shape[0]
    real_part = jnp.dot(
        select, jnp.asarray(table_re).reshape(16, 16), precision=lax.Precision.HIGHEST
    ).reshape(count, 4, 4)
    imag_part = jnp.dot(
        select, jnp.asarray(table_im).reshape(16, 16), precision=lax.Precision.HIGHEST
    ).reshape(count, 4, 4)
    return (real_part, imag_part)


def phases(momenta, first_site, count):
    index = first_site + jnp.arange(count, dtype=jnp.int32)
    coord_x = index // (LATT * LATT)
    coord_y = index // LATT % LATT
    coord_z = index % LATT
    phase_int = (
        momenta[:, 0:1] * coord_x[None, :]
        + momenta[:, 1:2] * coord_y[None, :]
        + momenta[:, 2:3] * coord_z[None, :]
    ) % LATT
    theta = 2.0 * math.pi / LATT * phase_int.astype(jnp.float32)
    return (jnp.cos(theta), jnp.sin(theta))


def left_side(vectors, cosine, sine_part):
    vec_re = vectors[0].astype(jnp.float32)[None]
    vec_im = vectors[1].astype(jnp.float32)[None]
    cosine = cosine[:, :, None, None]
    sine_part = sine_part[:, :, None, None]
    left_re = cosine * vec_re - sine_part * vec_im
    left_im = -(sine_part * vec_re + cosine * vec_im)
    return jnp.stack([left_re, left_im], 1).astype(jnp.bfloat16)


def right_side(vectors, gamma_re, gamma_im):
    count = vectors.shape[1]
    width = vectors.shape[3]
    sol_re = vectors[0].astype(jnp.float32).reshape(count, 4, 3, width)
    sol_im = vectors[1].astype(jnp.float32).reshape(count, 4, 3, width)
    high = lax.Precision.HIGHEST
    rot_re = jnp.einsum("gst,xtcj->gxscj", gamma_re, sol_re, precision=high) - jnp.einsum(
        "gst,xtcj->gxscj", gamma_im, sol_im, precision=high
    )
    rot_im = jnp.einsum("gst,xtcj->gxscj", gamma_re, sol_im, precision=high) + jnp.einsum(
        "gst,xtcj->gxscj", gamma_im, sol_re, precision=high
    )
    groups = gamma_re.shape[0]
    rot_re = rot_re.reshape(groups, count, 12, width)
    rot_im = rot_im.reshape(groups, count, 12, width)
    upper = jnp.stack([rot_re, rot_im], 3)
    lower = jnp.stack([-rot_im, rot_re], 3)
    return jnp.stack([upper, lower], 1).astype(jnp.bfloat16)


def general_body(eigvecs, solutions, momenta, gammas):
    local_sites = eigvecs.shape[1]
    vec_count = eigvecs.shape[3]
    col_count = solutions.shape[3]
    groups = gammas.shape[0]
    mom_count = momenta.shape[0]
    device = lax.axis_index("space")
    space_count = lax.axis_size("space")
    gamma_re, gamma_im = select_gammas(gammas)
    cosine, sine_part = phases(momenta, device * local_sites, local_sites)
    left = left_side(eigvecs, cosine, sine_part)
    right = right_side(solutions, gamma_re, gamma_im)
    partial_fields = jnp.einsum(
        "paxci,gaxcrj->gpirj", left, right, preferred_element_type=jnp.float32
    )
    partial_fields = partial_fields.reshape(groups * mom_count * vec_count, 2, col_count)
    fields = lax.psum_scatter(partial_fields, "space", scatter_dimension=0, tiled=True)
    own_rows = fields.shape[0]
    spacing = space_count // groups
    own_gamma = device // spacing
    row_index = device * own_rows + jnp.arange(own_rows, dtype=jnp.int32)
    row_mom = row_index % (mom_count * vec_count) // vec_count
    mom_onehot = (row_mom[:, None] == jnp.arange(mom_count, dtype=jnp.int32)[None, :]).astype(
        jnp.float32
    )
    gamma_range = jnp.arange(groups, dtype=jnp.int32)

    def pair_terms(first_rows, second_rows):
        real_sum = jnp.sum(
            first_rows[:, 0] * second_rows[:, 0] + first_rows[:, 1] * second_rows[:, 1], -1
        )
        imag_sum = jnp.sum(
            first_rows[:, 1] * second_rows[:, 0] - first_rows[:, 0] * second_rows[:, 1], -1
        )
        return jnp.dot(
            mom_onehot.T, jnp.stack([real_sum, imag_sum], 1), precision=lax.Precision.HIGHEST
        )

    def place(row_gamma, col_gamma, values):
        row_hot = (gamma_range == row_gamma).astype(jnp.float32)
        col_hot = (gamma_range == col_gamma).astype(jnp.float32)
        return row_hot[:, None, None, None] * col_hot[None, :, None, None] * values[None, None]

    total = place(own_gamma, own_gamma, pair_terms(fields, fields))
    last_shift = groups - 1
    for step in range(1, last_shift + 1):
        other = shifted(fields.astype(jnp.bfloat16), "space", step * spacing).astype(fields.dtype)
        values = pair_terms(fields, other)
        other_gamma = (own_gamma - step) % groups
        total = total + place(own_gamma, other_gamma, values)
    traces = lax.psum(total, ("space", "mode")) / float(vec_count * vec_count)
    return (fields, traces)


def solution(mesh):
    fits = dict(mesh.shape) == {"space": 16, "mode": 2}
    if fits:
        cut = Mesh(mesh.devices.reshape(4, 2, 2, 2), ("z", "x", "core", "mode"))
        space = ("z", "x", "core")
    else:
        cut, space = mesh, "space"

    def step(eigvecs, solutions, momenta, gammas):
        sized = eigvecs.shape == (2, 512, 12, 384) and solutions.shape == (2, 512, 12, 384)
        sized = sized and momenta.shape == (8, 3) and gammas.shape == (4,)
        return jax.shard_map(
            fast_body if fits and sized else general_body,
            mesh=cut if fits and sized else mesh,
            in_specs=(
                P(None, space if fits and sized else "space", None, None),
                P(None, space if fits and sized else "space", None, "mode"),
                P(),
                P(),
            ),
            out_specs=(P(space if fits and sized else "space", None, "mode"), P()),
            check_vma=False,
        )(eigvecs, solutions, momenta, gammas)

    return step
```

```python
import functools
import math

import jax
import jax.numpy as jnp
import numpy as np
from jax import lax
from jax.experimental import pallas as pl
from jax.experimental.pallas import tpu as pltpu
from jax.sharding import Mesh
from jax.sharding import PartitionSpec as P

LATT = 96
VMEM = pl.BlockSpec(memory_space=pltpu.VMEM)
SMEM = pl.BlockSpec(memory_space=pltpu.SMEM)
HBM = pl.BlockSpec(memory_space=pltpu.HBM)
BF16 = jnp.bfloat16
F32 = jnp.float32


ORDER = (6, 2, 4, 7, 3, 5, 1)
COST = pl.CostEstimate(flops=2_000_000_000, bytes_accessed=8_000_000, transcendentals=0)


def gamma_table():
    unit = 1j
    first = np.array([[0, 0, 0, unit], [0, 0, unit, 0], [0, -unit, 0, 0], [-unit, 0, 0, 0]])
    second = np.array([[0, 0, 0, -1], [0, 0, 1, 0], [0, 1, 0, 0], [-1, 0, 0, 0]], dtype=complex)
    third = np.array([[0, 0, unit, 0], [0, 0, 0, -unit], [-unit, 0, 0, 0], [0, unit, 0, 0]])
    fourth = np.array([[0, 0, 1, 0], [0, 0, 0, 1], [1, 0, 0, 0], [0, 1, 0, 0]], dtype=complex)
    basis = [first, second, third, fourth]
    table = []
    for number in range(16):
        matrix = np.eye(4, dtype=complex)
        for bit_pos in range(4):
            if number >> bit_pos & 1:
                matrix = matrix @ basis[bit_pos]
        table.append(matrix)
    return np.stack(table)


def shift_lanes(x, by):
    by = by % x.shape[-1]
    return x if by == 0 else pltpu.roll(x, by, x.ndim - 1)


def by_quarter(lane, first, second, third, fourth):
    tiles = []
    for k, (low, high) in enumerate(((first, second), (second, third), (third, fourth))):
        at = slice(k * 128, (k + 1) * 128)
        tiles.append(jnp.where(lane[:, at] < (k + 1) * 96, wide(low, at), wide(high, at)))
    return jnp.concatenate(tiles, axis=1)


def wide(x, at):
    return x[:, at] if x.shape[1] > 1 else x


def here():
    return lax.axis_index("z"), lax.axis_index("x"), lax.axis_index("core")


def prepare_sol_kernel(sol, sol_own, sol_other, turned):
    x = lax.axis_index("x")
    for r in range(2):
        flipped = sol[r].astype(F32).T.astype(BF16)
        for k in range(2):
            turned[k, :, r * 384 : (r + 1) * 384] = flipped[k * 96 : (k + 1) * 96]
    sol_own[...] = turned[x]
    sol_other[...] = turned[x ^ 1]


def prepare_sol(sol):
    return pl.pallas_call(
        prepare_sol_kernel,
        out_shape=[jax.ShapeDtypeStruct((96, 768), BF16)] * 2,
        in_specs=[VMEM],
        out_specs=[VMEM] * 2,
        scratch_shapes=[pltpu.VMEM((2, 96, 768), BF16)],
        compiler_params=pltpu.CompilerParams(vmem_limit_bytes=16 << 20),
        cost_estimate=COST,
    )(sol)


def prepare_eig_kernel(eig, after, full, *rest):
    eig_out, packs = rest[:3], rest[3]
    z, half = lax.axis_index("z"), lax.axis_index("mode")
    lane = lax.broadcasted_iota(jnp.int32, (96, 384), 1)
    for side in range(2):
        at = side * 192
        parts = [
            eig[r, at + low * 96 : at + low * 96 + 96, :].astype(F32)
            for low in range(2)
            for r in range(2)
        ]
        for quarter in range(4):
            moved = [shift_lanes(part, 96 * (k - quarter)) for k, part in enumerate(parts)]
            packs[quarter, side] = by_quarter(lane, *moved).astype(BF16)
    full[0:96] = packs[z, 0]
    full[96:192] = packs[z, 1]
    for k in range(1, 4):
        eig_out[k - 1][...] = packs[z ^ k, half]


def site_phases(momenta, cosine, sine):
    z, x, core = here()
    shape = cosine.shape[::-1]
    mom = lax.broadcasted_iota(jnp.int32, shape, 0)
    lane = lax.broadcasted_iota(jnp.int32, shape, 1)
    device = (z * 4 + x * 2 + core) ^ ((lane >> 5) << 1)
    site = (device * 32 + (lane & 31)).astype(F32)
    line = jnp.floor((site + 0.5) * (1.0 / LATT))
    coord_x = jnp.floor((line + 0.5) * (1.0 / LATT))
    coords = (coord_x, line - LATT * coord_x, site - LATT * line)
    steps = jnp.zeros(shape, F32)
    for axis, coord in enumerate(coords):
        factor = jnp.zeros(shape, F32)
        for p in range(8):
            factor = jnp.where(mom == p, momenta[axis, p].astype(F32), factor)
        steps += factor * coord
    steps -= LATT * jnp.floor((steps + 0.5) * (1.0 / LATT))
    theta = 2.0 * math.pi / LATT * steps
    cosine[...] = jnp.cos(theta).T
    sine[...] = jnp.sin(theta).T


def prepare_eig(eig, after):
    return pl.pallas_call(
        prepare_eig_kernel,
        out_shape=[jax.ShapeDtypeStruct((192, 384), BF16)]
        + [jax.ShapeDtypeStruct((96, 384), BF16)] * 3,
        in_specs=[VMEM, HBM],
        out_specs=[VMEM] * 4,
        scratch_shapes=[pltpu.VMEM((4, 2, 96, 384), BF16)],
        compiler_params=pltpu.CompilerParams(vmem_limit_bytes=16 << 20),
    )(eig, after)


def build_base(first, second, base):
    lane = lax.broadcasted_iota(jnp.int32, (96, 384), 1)
    parts = [
        [plane[m, :, r * 384 : (r + 1) * 384] for plane in (first, second) for m in range(2)]
        for r in range(2)
    ]
    for t in range(4):
        re, im = [
            by_quarter(lane, *[shift_lanes(x, 96 * (k - t)) for k, x in enumerate(part)])
            for part in parts
        ]
        for turn, x in enumerate((re, -im, -re, im)):
            base[turn * 4 + t] = x


def build_left(base, gammas, table, left):
    for g in range(4):
        for part in range(2):
            at = g * 192 + part * 96
            for s in range(4):
                source = table[gammas[g] * 8 + part * 4 + s]
                left[at : at + 96, s * 384 : (s + 1) * 384] = base[source]


def build_phases(cosine, sine, at, phases):
    lane = lax.broadcasted_iota(jnp.int32, (32, 384), 1)
    for part, table in enumerate((cosine, sine)):
        rows = table[at : at + 32, :]
        for h in range(2):
            four = [rows[:, p : p + 1] for p in (2 * h, 2 * h + 1, 2 * h + 4, 2 * h + 5)]
            phases[h, part] = by_quarter(lane, *four)


def build_right(blocks, k, m, cosine, sine, right, phases, spread):
    lane = lax.broadcasted_iota(jnp.int32, (96, 384), 1)
    build_phases(cosine, sine, (k * 2 + m) * 32, phases)
    for spin, block in blocks:
        w = block.astype(F32)
        turns = [shift_lanes(w, 96 * by) for by in range(4)]
        copies = [
            by_quarter(lane, *[turns[(k4 - part) % 4] for k4 in range(4)]).reshape(3, 32, 384)
            for part in range(4)
        ]
        for low in range(2):
            re, im = copies[low * 2], -copies[low * 2 + 1]
            for h in range(2):
                cos, sin = phases[h, 0][None], phases[h, 1][None]
                at = (spin + low) * 384 + (k % 2) * 192 + m * 96
                rows = slice(at, at + 96)
                right[h, rows, 0:384] = (cos * re + sin * im).reshape(96, 384).astype(BF16)
                right[h, rows, 384:768] = (cos * im - sin * re).reshape(96, 384).astype(BF16)


def far_blocks(eigs, k, m):
    x = lax.axis_index("x")
    return [(half * 2, eigs[x ^ m, half, k - 1]) for half in range(2)]


def product(left, right, side, n):
    at = slice(n * 256, (n + 1) * 256)
    return at, jnp.dot(left[...], right[side, :, at], preferred_element_type=F32)


def near_kernel(gammas, table, momenta, *refs):
    sols, fulls, eigs, accs, far_right = refs[:2], refs[2:4], refs[4], refs[5:7], refs[7]
    base, left, right, phases, spread, cosine, sine = refs[8:]
    site_phases(momenta, cosine, sine)
    work = (phases, spread)
    for m in range(2):
        blocks = [(0, fulls[m][0:96]), (2, fulls[m][96:192])]
        build_right(blocks, 0, m, cosine, sine, right, *work)
    build_base(*sols, base)
    build_left(base, gammas, table, left)
    for k in range(1, 4):
        for m in range(2):
            build_right(far_blocks(eigs, k, m), k, m, cosine, sine, far_right if k > 1 else right, *work)
    core = lax.axis_index("core")
    for acc, side in ((accs[0], core), (accs[1], core ^ 1)):
        for n in range(3):
            at, part = product(left, right, side, n)
            acc[:, at] = part


def given_kernel(gammas, table, second, first, right, acc, out, left, base):
    build_base(first, second, base)
    build_left(base, gammas, table, left)
    for n in range(2):
        at, part = product(left, right, lax.axis_index("core") ^ 1, n)
        out[:, at] = (acc[:, at] + part).astype(BF16)


def rest_kernel(left, right, acc, out):
    at, part = product(left, right, lax.axis_index("core") ^ 1, 2)
    out[...] = (acc[:, at] + part).astype(BF16)


def own_kernel(left, right, acc, out):
    for n in range(3):
        at, part = product(left, right, lax.axis_index("core"), n)
        out[:, at] = acc[:, at] + part


def finish_kernel(own, got, got_rest, *rest):
    outs, pairs = rest[:8], rest[8]
    z, x, _ = here()
    low = lax.broadcasted_iota(jnp.int32, (96, 384), 1) < 192
    gs, res, ims = [z ^ k for k in range(4)], [], []
    for k in range(4):
        (a, b), (c, d) = [
            [
                own[pl.ds(at, 96), :384] + got[pl.ds(at, 96), :384].astype(F32),
                own[pl.ds(at, 96), 384:]
                + jnp.concatenate(
                    [got[pl.ds(at, 96), 384:].astype(F32), got_rest[pl.ds(at, 96), :].astype(F32)],
                    axis=1,
                ),
            ]
            for at in (pl.multiple_of(gs[k] * 192, 96), pl.multiple_of(gs[k] * 192 + 96, 96))
        ]
        re, im = a - d, b + c
        res.append(re)
        ims.append(im)
        first = jnp.where(low, re, shift_lanes(im, 192))
        second = jnp.where(low, shift_lanes(re, 192), im)
        for tile in range(3):
            lanes, rows = slice(tile * 128, (tile + 1) * 128), slice(tile * 96, (tile + 1) * 96)
            one, two = first[:, lanes], second[:, lanes]
            outs[k * 2][rows] = jnp.where(x == 0, one, two).astype(BF16)
            outs[k * 2 + 1][rows] = jnp.where(x == 0, two, one).astype(BF16)
    for i in range(4):
        for k in range(i, 4):
            at, mirror = (gs[i] * 4 + gs[k]) * 2, (gs[k] * 4 + gs[i]) * 2
            both = jnp.sum(res[i] * res[k] + ims[i] * ims[k], axis=0, keepdims=True)
            pairs[pl.ds(at, 1), :] = both
            if k > i:
                turn = jnp.sum(ims[i] * res[k] - res[i] * ims[k], axis=0, keepdims=True)
                pairs[pl.ds(mirror, 1), :] = both
                pairs[pl.ds(at + 1, 1), :] = turn
                pairs[pl.ds(mirror + 1, 1), :] = -turn
            else:
                pairs[pl.ds(at + 1, 1), :] = jnp.zeros_like(both)
    lane_p = lax.broadcasted_iota(jnp.int32, (8, 384), 1)
    mom = lax.broadcasted_iota(jnp.int32, (8, 384), 0)
    total = lax.dot_general(
        (lane_p // 96 == mom).astype(F32),
        pairs[...],
        (((1,), (1,)), ((), ())),
        precision=lax.Precision.HIGHEST,
        preferred_element_type=F32,
    )
    high = total.astype(BF16)
    low_part = (total - high.astype(F32)).astype(BF16)
    tail = jnp.concatenate([high, low_part, jnp.zeros((8, 64), BF16)], axis=1)
    for k in range(8):
        outs[k][288:296] = tail


BASE = pltpu.VMEM((16, 96, 384), BF16)
SPREAD = [pltpu.VMEM((2, 2, 32, 384), F32), pltpu.VMEM((2, 4, 96, 384), F32)]


def call(kernel, inputs, scalars, out_shape, scratch=(), limit=24):
    return pl.pallas_call(
        kernel,
        out_shape=out_shape,
        in_specs=[SMEM] * len(scalars) + [VMEM] * len(inputs),
        out_specs=jax.tree.map(lambda _: VMEM, out_shape),
        scratch_shapes=scratch,
        compiler_params=pltpu.CompilerParams(vmem_limit_bytes=limit << 20),
    )(*scalars, *inputs)


def join_kernel(*refs):
    got, out, blocks = refs[:8], refs[8], refs[9]
    z, x, _ = here()
    for k, block in zip((0,) + ORDER, got):
        for tile in range(3):
            lanes = slice(tile * 128, (tile + 1) * 128)
            blocks[(z ^ (k // 2)) * 2 + (x ^ (k % 2)), :, lanes] = block[tile * 96 : tile * 96 + 96]
    for side in range(2):
        rows = slice(side * 96, (side + 1) * 96)
        parts = [blocks[k * 2 + side].astype(F32) for k in range(4)]
        for r in range(2):
            for p in range(2):
                at = r * 192 + p * 96
                out[r, rows, p * 384 : (p + 1) * 384] = jnp.concatenate(
                    [part[:, at : at + 96] for part in parts], axis=1
                )


def traces_kernel(vec_count, own, core, own_mode, core_mode, out):
    mine, other = own[...] + own_mode[...], core[...] + core_mode[...]
    first = lax.axis_index("core") == 0
    low, high = jnp.where(first, mine, other), jnp.where(first, other, mine)
    rows = jnp.concatenate([low[0:2], high[0:2], low[2:4], high[2:4]], axis=0)
    rows = rows * (1.0 / float(vec_count * vec_count))
    turned = jnp.concatenate([rows, jnp.zeros((8, 96), F32)], axis=1).T
    for g in range(4):
        for k in range(4):
            at = (g * 4 + k) * 2
            out[g, k] = turned[at : at + 2]


def swap(x, axis, mask):
    return lax.ppermute(x, axis, [(i, i ^ mask) for i in range(lax.axis_size(axis))])


def fast_body(eigvecs, solutions, momenta, gammas):
    vec_count = eigvecs.shape[3]
    eig = eigvecs.transpose(0, 2, 1, 3).reshape(2, 384, 384)
    sol = solutions.transpose(0, 2, 1, 3).reshape(2, 384, 192)
    sol_own, sol_other = prepare_sol(sol)
    full, *eig_own = prepare_eig(eig, sol_other)
    sol_pair = jnp.stack([sol_own, swap(sol_other, "x", 1)])
    mine = jnp.stack([swap(eig_own[k - 1], "z", k) for k in range(1, 4)])
    sols = [sol_pair] + [swap(sol_pair, "z", k) for k in range(1, 4)]

    table = gamma_table()
    spin = np.argmax(np.abs(table), axis=2)
    turn = np.round(np.angle(table.sum(axis=2)) / (np.pi / 2)).astype(int) % 4
    rows = np.stack([turn * 4 + spin, (turn + 3) % 4 * 4 + spin], axis=1)
    scalars = (gammas, jnp.asarray(rows.astype(np.int32).reshape(128)))

    total = jax.ShapeDtypeStruct((768, 768), F32)
    left, right = pltpu.VMEM((768, 1536), BF16), (2, 1536, 768)
    eig_all = lax.all_gather(mine, ("x", "mode")).reshape(2, 2, 3, 96, 384)
    acc_own, acc_other, right = call(
        near_kernel,
        [*sols[:2], full, swap(full, "x", 1), eig_all],
        [*scalars, momenta.T],
        [total] * 2 + [jax.ShapeDtypeStruct(right, BF16)],
        [
            BASE,
            left,
            pltpu.VMEM(right, BF16),
            *SPREAD,
            pltpu.VMEM((256, 8), F32),
            pltpu.VMEM((256, 8), F32),
        ],
        36,
    )
    given, left = call(
        given_kernel,
        [sols[3], sols[2], right, acc_other],
        scalars,
        [jax.ShapeDtypeStruct((768, 512), BF16), jax.ShapeDtypeStruct((768, 1536), BF16)],
        [BASE],
    )
    given_rest = call(
        rest_kernel, [left, right, acc_other], [], jax.ShapeDtypeStruct((768, 256), BF16)
    )
    taken = [swap(given, "core", 1), swap(given_rest, "core", 1)]
    own = call(own_kernel, [left, right, acc_own], [], total)
    sent = call(
        finish_kernel,
        [own, *taken],
        [],
        [jax.ShapeDtypeStruct((296, 128), BF16)] * 8,
        [pltpu.VMEM((32, 384), F32)],
    )
    got = [sent[0]] + [swap(sent[k], ("z", "x"), k) for k in ORDER]
    part = sum(block[288:292, :64].astype(F32) for block in got)
    part = part[:, :32] + part[:, 32:]
    others = [swap(part, "core", 1), swap(part, "mode", 1), swap(part, ("core", "mode"), 3)]
    traces = call(
        functools.partial(traces_kernel, vec_count),
        [part, *others],
        [],
        jax.ShapeDtypeStruct((4, 4, 2, 8), F32),
    ).transpose(0, 1, 3, 2)
    fields = call(
        join_kernel,
        got,
        [],
        jax.ShapeDtypeStruct((2, 192, 768), F32),
        [pltpu.VMEM((8, 96, 384), BF16)],
    ).transpose(2, 0, 1)
    return fields, traces


def shifted(x, axis, by):
    count = lax.axis_size(axis)
    return lax.ppermute(x, axis, [(i, (i + by) % count) for i in range(count)])


def select_gammas(gammas):
    table = gamma_table()
    table_re, table_im = table.real.astype(np.float32), table.imag.astype(np.float32)
    select = (gammas[:, None] == jnp.arange(16, dtype=jnp.int32)[None, :]).astype(jnp.float32)
    count = gammas.shape[0]
    real_part = jnp.dot(
        select, jnp.asarray(table_re).reshape(16, 16), precision=lax.Precision.HIGHEST
    ).reshape(count, 4, 4)
    imag_part = jnp.dot(
        select, jnp.asarray(table_im).reshape(16, 16), precision=lax.Precision.HIGHEST
    ).reshape(count, 4, 4)
    return (real_part, imag_part)


def phases(momenta, first_site, count):
    index = first_site + jnp.arange(count, dtype=jnp.int32)
    coord_x = index // (LATT * LATT)
    coord_y = index // LATT % LATT
    coord_z = index % LATT
    phase_int = (
        momenta[:, 0:1] * coord_x[None, :]
        + momenta[:, 1:2] * coord_y[None, :]
        + momenta[:, 2:3] * coord_z[None, :]
    ) % LATT
    theta = 2.0 * math.pi / LATT * phase_int.astype(jnp.float32)
    return (jnp.cos(theta), jnp.sin(theta))


def left_side(vectors, cosine, sine_part):
    vec_re = vectors[0].astype(jnp.float32)[None]
    vec_im = vectors[1].astype(jnp.float32)[None]
    cosine = cosine[:, :, None, None]
    sine_part = sine_part[:, :, None, None]
    left_re = cosine * vec_re - sine_part * vec_im
    left_im = -(sine_part * vec_re + cosine * vec_im)
    return jnp.stack([left_re, left_im], 1).astype(jnp.bfloat16)


def right_side(vectors, gamma_re, gamma_im):
    count = vectors.shape[1]
    width = vectors.shape[3]
    sol_re = vectors[0].astype(jnp.float32).reshape(count, 4, 3, width)
    sol_im = vectors[1].astype(jnp.float32).reshape(count, 4, 3, width)
    high = lax.Precision.HIGHEST
    rot_re = jnp.einsum("gst,xtcj->gxscj", gamma_re, sol_re, precision=high) - jnp.einsum(
        "gst,xtcj->gxscj", gamma_im, sol_im, precision=high
    )
    rot_im = jnp.einsum("gst,xtcj->gxscj", gamma_re, sol_im, precision=high) + jnp.einsum(
        "gst,xtcj->gxscj", gamma_im, sol_re, precision=high
    )
    groups = gamma_re.shape[0]
    rot_re = rot_re.reshape(groups, count, 12, width)
    rot_im = rot_im.reshape(groups, count, 12, width)
    upper = jnp.stack([rot_re, rot_im], 3)
    lower = jnp.stack([-rot_im, rot_re], 3)
    return jnp.stack([upper, lower], 1).astype(jnp.bfloat16)


def general_body(eigvecs, solutions, momenta, gammas):
    local_sites = eigvecs.shape[1]
    vec_count = eigvecs.shape[3]
    col_count = solutions.shape[3]
    groups = gammas.shape[0]
    mom_count = momenta.shape[0]
    device = lax.axis_index("space")
    space_count = lax.axis_size("space")
    gamma_re, gamma_im = select_gammas(gammas)
    cosine, sine_part = phases(momenta, device * local_sites, local_sites)
    left = left_side(eigvecs, cosine, sine_part)
    right = right_side(solutions, gamma_re, gamma_im)
    partial_fields = jnp.einsum(
        "paxci,gaxcrj->gpirj", left, right, preferred_element_type=jnp.float32
    )
    partial_fields = partial_fields.reshape(groups * mom_count * vec_count, 2, col_count)
    fields = lax.psum_scatter(partial_fields, "space", scatter_dimension=0, tiled=True)
    own_rows = fields.shape[0]
    spacing = space_count // groups
    own_gamma = device // spacing
    row_index = device * own_rows + jnp.arange(own_rows, dtype=jnp.int32)
    row_mom = row_index % (mom_count * vec_count) // vec_count
    mom_onehot = (row_mom[:, None] == jnp.arange(mom_count, dtype=jnp.int32)[None, :]).astype(
        jnp.float32
    )
    gamma_range = jnp.arange(groups, dtype=jnp.int32)

    def pair_terms(first_rows, second_rows):
        real_sum = jnp.sum(
            first_rows[:, 0] * second_rows[:, 0] + first_rows[:, 1] * second_rows[:, 1], -1
        )
        imag_sum = jnp.sum(
            first_rows[:, 1] * second_rows[:, 0] - first_rows[:, 0] * second_rows[:, 1], -1
        )
        return jnp.dot(
            mom_onehot.T, jnp.stack([real_sum, imag_sum], 1), precision=lax.Precision.HIGHEST
        )

    def place(row_gamma, col_gamma, values):
        row_hot = (gamma_range == row_gamma).astype(jnp.float32)
        col_hot = (gamma_range == col_gamma).astype(jnp.float32)
        return row_hot[:, None, None, None] * col_hot[None, :, None, None] * values[None, None]

    total = place(own_gamma, own_gamma, pair_terms(fields, fields))
    last_shift = groups - 1
    for step in range(1, last_shift + 1):
        other = shifted(fields.astype(jnp.bfloat16), "space", step * spacing).astype(fields.dtype)
        values = pair_terms(fields, other)
        other_gamma = (own_gamma - step) % groups
        total = total + place(own_gamma, other_gamma, values)
    traces = lax.psum(total, ("space", "mode")) / float(vec_count * vec_count)
    return (fields, traces)


def solution(mesh):
    fits = dict(mesh.shape) == {"space": 16, "mode": 2}
    if fits:
        cut = Mesh(mesh.devices.reshape(4, 2, 2, 2), ("z", "x", "core", "mode"))
        space = ("z", "x", "core")
    else:
        cut, space = mesh, "space"

    def step(eigvecs, solutions, momenta, gammas):
        sized = eigvecs.shape == (2, 512, 12, 384) and solutions.shape == (2, 512, 12, 384)
        sized = sized and momenta.shape == (8, 3) and gammas.shape == (4,)
        return jax.shard_map(
            fast_body if fits and sized else general_body,
            mesh=cut if fits and sized else mesh,
            in_specs=(
                P(None, space if fits and sized else "space", None, None),
                P(None, space if fits and sized else "space", None, "mode"),
                P(),
                P(),
            ),
            out_specs=(P(space if fits and sized else "space", None, "mode"), P()),
            check_vma=False,
        )(eigvecs, solutions, momenta, gammas)

    return step
```
